512 devices in a mesh: row: 128 (over y_hi, x, z), head: 4 (over y_lo, core).
Axes of the slice: x: 4, y: 4 (y_hi: 2, y_lo: 2; y = y_hi * 2 + y_lo), z: 16, core: 2. Of those that a mesh axis runs over, the one named last changes fastest.
Arguments:
- pair: bfloat16 [512, 512, 128], P('row', None, 'head'), may hold values from -100 to 100
- w_query: bfloat16 [128, 128], P(None, 'head'), may hold values from -0.5 to 0.5
- w_key: bfloat16 [128, 128], P(None, 'head'), may hold values from -0.5 to 0.5
- w_value: bfloat16 [128, 128], P(None, 'head'), may hold values from -0.5 to 0.5
- w_gate: bfloat16 [128, 128], P(None, 'head'), may hold values from -0.5 to 0.5
- w_bias: bfloat16 [128, 4], P(None, 'head')
- w_out: bfloat16 [128, 128], replicated, may hold values from -0.5 to 0.5
- intra_chain_logit_shift: float32 [4], P('head'), may hold values from -2 to 2
- block_lists: int32 [8, 2], replicated, may hold values from 0 to 7, as said below
- chain_ids: int32 [512], replicated, may hold values from 0 to 3, never falling along the last dimension, each value on 1 to 256 neighbouring positions
Outputs:
- attended: bfloat16 [512, 512, 128], P(None, ('row', 'head'))
The draws below stay inside these ranges and needn't reach their ends.
Inputs may be any that keep to these rules, and one draw needn't show every extreme that they name: `block_lists`: each query block b lists 2 distinct key blocks in rising order, b itself among them.
All inputs are finite; a program needn't handle non-finite values.
Results may differ from the reference program's by a relative error of at most 0.012.
The reference program's roundings to bfloat16 on the way count: a program that leaves them out, or rounds other values in their place, can miss the bound.
Values may be sent and summed in bfloat16 or wider, within the bound.
No kernel may reach another device: no remote copies, remote signals or barrier semaphores. Data moves between devices by JAX's collectives and lax.ppermute only.
A program may use at most 64 MiB of HBM per device.

```python
import math
import jax
import jax.numpy as jnp
import numpy as np
from jax import lax

C = 128
H = 4
HD = 32
NBLK = 8
KB = 2
N = 512
BLK = 64


def draw_pair(key, part):
    value = jax.random.truncated_normal(jax.random.fold_in(key, 1), -6.0, 6.0, (N, N, C), jnp.float32)
    return value.astype(jnp.bfloat16)


def draw_w_bias(key, part):
    value = jax.random.normal(jax.random.fold_in(key, 6), (C, H), jnp.float32) / math.sqrt(C)
    return value.astype(jnp.bfloat16)


def draw_block_lists(key, part):
    key_rows = jax.random.split(jax.random.fold_in(key, 21), NBLK)
    perms = jax.vmap(lambda one: jax.random.permutation(one, NBLK - 1))(key_rows)[:, :KB - 1] + 1
    offsets = jnp.concatenate([jnp.zeros((NBLK, 1), jnp.int32), perms.astype(jnp.int32)], axis=1)
    lists = (jnp.arange(NBLK, dtype=jnp.int32)[:, None] + offsets) % NBLK
    return jnp.sort(lists, axis=1).astype(jnp.int32)


def levels(stream_key, extent, cuts, smallest, top_value):
    gain = 1.0
    for position, parts in cuts:
        heights = jax.random.uniform(jax.random.fold_in(jax.random.fold_in(stream_key, 6), position), (parts,), jnp.float32, smallest / len(cuts), top_value / len(cuts))
        gain = gain * jnp.repeat(jnp.exp(heights), extent[position] // parts).reshape((-1,) + (1,) * (len(extent) - 1 - position))
    return gain


def split_up(amount, total, most, slope):
    loads = [(1 << 20) // math.isqrt(standing ** slope) + 1 for standing in range(2, amount + 1)]
    surplus, counts = total - most - (amount - 1), [1] * (amount - 1)
    while surplus > 0:
        free = [i for i in range(amount - 1) if counts[i] < most]
        pool, budget = sum([loads[i] for i in free]), surplus
        for i in free:
            addition = min(most - counts[i], max(1, budget * loads[i] // pool), surplus)
            counts[i] = counts[i] + addition
            surplus = surplus - addition
    return np.array([most] + counts)


def ragged_sizes(own_key, count, total, bound, lean):
    if count == 2:
        one = jax.random.randint(own_key, (), max(1, total - bound), min(bound, total - 1) + 1)
        return jnp.stack([one, total - one])
    lengths = jnp.asarray(split_up(count, total, bound, lean), jnp.int32)
    twos = (count - 1) // 2
    giver, receiver = lengths[1:1 + 2 * twos:2], lengths[2:2 + 2 * twos:2]
    room = jnp.minimum(giver - 1, bound - receiver)
    passed = jax.random.randint(jax.random.fold_in(own_key, 1), (twos,), 0, 1 << 20) % (room + 1)
    lengths = lengths.at[1:1 + 2 * twos:2].set(giver - passed).at[2:2 + 2 * twos:2].set(receiver + passed)
    return lengths[jax.random.permutation(jax.random.fold_in(own_key, 2), count)]


def scatter_about(stream_key, shape, width, most, cuts=(), kind=jnp.bfloat16):
    array = width * jax.random.normal(stream_key, shape, jnp.float32)
    if cuts:
        array = array * levels(stream_key, shape, cuts, -0.22, 0.18)
    return jnp.clip(array, -most, most).astype(kind)


def setup_inputs(seed: int = 0) -> dict:
    key_of = jax.random.split(jax.random.key(seed), 11)
    pair = draw_pair(jax.random.fold_in(key_of[10], 71), 0)
    w_query = scatter_about(key_of[1], (C, H * HD), C ** -0.5, 0.5, ((1, 4),))
    w_key = scatter_about(key_of[2], (C, H * HD), C ** -0.5, 0.5, ((1, 4),))
    w_value = scatter_about(key_of[3], (C, H * HD), C ** -0.5, 0.5, ((1, 4),))
    w_gate = scatter_about(key_of[4], (C, H * HD), C ** -0.5, 0.5, ((1, 4),))
    w_bias = draw_w_bias(jax.random.fold_in(key_of[10], 71), 0)
    w_out = scatter_about(key_of[6], (H * HD, C), (H * HD) ** -0.5, 0.5)
    intra_chain_logit_shift = jnp.clip(jax.random.uniform(key_of[7], (H,), jnp.float32, -2.0, 2.0) * levels(key_of[7], (H,), ((0, 4),), -0.4, 0.0), -2.0, 2.0)
    block_lists = draw_block_lists(jax.random.fold_in(key_of[10], 71), 0)
    chain_ids = jnp.searchsorted(jnp.cumsum(ragged_sizes(key_of[9], 4, N, N // 2, 2)), jnp.arange(N), side="right").astype(jnp.int32)
    return {"pair": pair, "w_query": w_query, "w_key": w_key, "w_value": w_value, "w_gate": w_gate, "w_bias": w_bias, "w_out": w_out, "intra_chain_logit_shift": intra_chain_logit_shift, "block_lists": block_lists, "chain_ids": chain_ids}


def reference(pair, w_query, w_key, w_value, w_gate, w_bias, w_out, intra_chain_logit_shift, block_lists, chain_ids):
    plane = jnp.dot(pair.reshape(N * N, C), w_bias, preferred_element_type=jnp.float32).astype(jnp.bfloat16)
    plane = plane.reshape(N, N, H).transpose(2, 0, 1).reshape(H, NBLK, BLK, NBLK, BLK)
    picked = jnp.take_along_axis(plane, block_lists[None, :, None, :, None], axis=3)
    picked = picked.reshape(H, NBLK, BLK, KB * BLK).astype(jnp.float32)
    key_pos = (block_lists[:, :, None] * BLK + jnp.arange(BLK, dtype=jnp.int32)[None, None, :]).reshape(NBLK, KB * BLK)
    same = chain_ids.reshape(NBLK, BLK)[:, :, None] == jnp.take(chain_ids, key_pos)[:, None, :]
    logit_bias = picked + intra_chain_logit_shift[:, None, None, None] * same.astype(jnp.float32)[None]
    w_all = jnp.concatenate([w_query, w_key, w_value, w_gate], axis=1)
    logit_scale = 1.0 / math.sqrt(HD)

    def one_row(zrow):
        projected = jnp.dot(zrow, w_all, preferred_element_type=jnp.float32).astype(jnp.bfloat16)
        projected = projected.reshape(N, 4, H, HD).transpose(1, 2, 0, 3)
        query_rows = projected[0].reshape(H, NBLK, BLK, HD).astype(jnp.float32)
        key_rows = jnp.take(projected[1], key_pos, axis=1).astype(jnp.float32)
        value_rows = jnp.take(projected[2], key_pos, axis=1).astype(jnp.float32)
        scores = jnp.einsum('hbqd,hbkd->hbqk', query_rows, key_rows) * logit_scale + logit_bias
        top = lax.optimization_barrier(jnp.max(scores, axis=-1, keepdims=True))
        expo = jnp.exp(scores - top)
        attention_weight = (expo / lax.optimization_barrier(jnp.sum(expo, axis=-1, keepdims=True))).astype(jnp.bfloat16)
        mixed = jnp.einsum('hbqk,hbkd->hbqd', attention_weight.astype(jnp.float32), value_rows).reshape(H, N, HD)
        gated = (jax.nn.sigmoid(projected[3].astype(jnp.float32)) * mixed).astype(jnp.bfloat16)
        gated = gated.transpose(1, 0, 2).reshape(N, H * HD)
        return jnp.dot(gated, w_out, preferred_element_type=jnp.float32).astype(jnp.bfloat16)
    return lax.map(one_row, pair)
```

```python
import functools
import math

import jax
import jax.numpy as jnp
from jax import lax
from jax.experimental import pallas as pl
from jax.experimental.pallas import tpu as pltpu
from jax.sharding import PartitionSpec as P

F32, BF16 = jnp.float32, jnp.bfloat16
VMEM = pl.BlockSpec(memory_space=pltpu.VMEM)
SMEM = pl.BlockSpec(memory_space=pltpu.SMEM)
LIMIT = 24 * 1024 * 1024
BLK, NBLK, HEADS, HD, C, N = 64, 8, 4, 32, 128, 512
ROWS = 4
QB = 16


def nt(a, b):
    return lax.dot_general(a, b, (((1,), (1,)), ((), ())), preferred_element_type=F32)


def nn(a, b):
    return jnp.dot(a, b, preferred_element_type=F32)


def iota(shape, dim):
    return lax.broadcasted_iota(jnp.int32, shape, dim)


def pack_kernel(pair, wq, wk, wv, wg, wb, shift, out):
    h = lax.axis_index("head")
    out[0:128, :] = pair[...].reshape(128, N)
    out[128:160, 0:128] = wq[...]
    out[128:160, 128:256] = wk[...]
    out[128:160, 256:384] = wv[...]
    out[128:160, 384:512] = wg[...]
    s = jnp.full((16, 128), shift[0], F32)
    hi = s.astype(BF16).astype(F32)
    mid = (s - hi).astype(BF16).astype(F32)
    low = s - hi - mid
    w = jnp.broadcast_to(wb[...].astype(F32), (16, 128))
    row = iota((16, 128), 0)
    part = row // 4
    value = jnp.where(part == 0, w, jnp.where(part == 1, hi, jnp.where(part == 2, mid, low)))
    value = jnp.where(row % 4 == h, value, 0.0)
    out[160:176, 0:128] = value.astype(BF16)
    out[160:176, 128:512] = jnp.zeros((16, 384), BF16)


def heads_small(g):
    small = g[0, 160:176, 0:128].astype(F32)
    for k in range(1, HEADS):
        small = small + g[k, 160:176, 0:128].astype(F32)
    return small


def pick(first, second, b0, b1):
    lane = iota(first.shape, 1)
    first = jnp.where(b0 % 2 == 0, first, pltpu.roll(first, 64, 1))
    second = jnp.where(b1 % 2 == 1, second, pltpu.roll(second, 64, 1))
    return jnp.where(lane < 64, first, second)


def bias_kernel(lists, g, out):
    h = lax.axis_index("head")
    b = lax.axis_index("row") // 16
    small = heads_small(g).astype(BF16)
    found = []
    for s in range(2):
        chunk = pl.multiple_of(lists[b, s] // 2 * 128, 128)
        z = jnp.concatenate(
            [g[k, pl.ds(pl.multiple_of(h * 32, 32), 32), pl.ds(chunk, 128)] for k in range(HEADS)], axis=0
        )
        found.append(nn(small, z))
    both = pick(found[0], found[1], lists[b, 0], lists[b, 1])[0:4]
    tile = jnp.concatenate([both] * 4, axis=0).astype(BF16)
    for r in range(32):
        out[r * 16 : (r + 1) * 16, :] = tile


def score_kernel(lists, chain, g, s_out, v_out, g_out, k_scr):
    h = lax.axis_index("head")
    small = heads_small(g)
    sel = (iota((128, N), 1) == 4 * iota((128, N), 0) + h).astype(BF16)
    wT = jnp.concatenate([g[k, 128:160, :] for k in range(HEADS)], axis=0)
    w_qg = jnp.concatenate([wT[:, 0:128], wT[:, 384:512]], axis=0)
    w_kv = wT[:, 128:384]
    w_kv = jnp.concatenate([w_kv[:, 0:128], w_kv[:, 128:256]], axis=0)
    chain_q = nt(sel, jnp.broadcast_to(chain[...].astype(F32).astype(BF16), (128, N)))
    scale = 1.0 / math.sqrt(HD)
    lane16 = iota((QB, 128), 1) // HD
    same = []
    for b in range(NBLK):
        b0, b1 = lists[b, 0], lists[b, 1]
        c0 = chain[:, pl.ds(pl.multiple_of(b0 // 2 * 128, 128), 128)].astype(F32)
        c1 = chain[:, pl.ds(pl.multiple_of(b1 // 2 * 128, 128), 128)].astype(F32)
        ck = pick(jnp.broadcast_to(c0, (8, 128)), jnp.broadcast_to(c1, (8, 128)), b0, b1)[0:1]
        same.append(chain_q[b * QB : (b + 1) * QB] == ck)
    shifts = [small[4 + k : 5 + k] + small[8 + k : 9 + k] + small[12 + k : 13 + k] for k in range(HEADS)]
    for i in range(ROWS):
        zt = jnp.concatenate([g[k, i * 32 : (i + 1) * 32, :] for k in range(HEADS)], axis=0)
        z = zt.T
        kv = nt(z, w_kv).astype(BF16)
        k_scr[i] = kv[:, 0:128]
        v_out[i] = kv[:, 128:256]
        zq = nt(sel, zt).astype(BF16)
        qg = nt(zq, w_qg).astype(BF16)
        g_out[i] = qg[:, 128:256]
        q = qg[:, 0:128]
        for b in range(NBLK):
            q16 = q[b * QB : (b + 1) * QB]
            zero = jnp.zeros_like(q16)
            qbd = jnp.concatenate([jnp.where(lane16 == k, q16, zero) for k in range(HEADS)], axis=0)
            kb = jnp.concatenate(
                [k_scr[i, pl.ds(pl.multiple_of(lists[b, s] * BLK, BLK), BLK), :] for s in range(2)], axis=0
            )
            s64 = nt(qbd, kb) * scale
            for k in range(HEADS):
                s_out[i, b, k * QB : (k + 1) * QB, :] = s64[k * QB : (k + 1) * QB] + jnp.where(same[b], shifts[k], 0.0)


def mix_kernel(lists, bias, s_in, v, gate, w_out, out, acc):
    perm = (iota((64, 64), 1) == (iota((64, 64), 0) % QB) * 4 + iota((64, 64), 0) // QB).astype(BF16)
    lane16 = iota((QB, 128), 1) // HD
    for b in range(NBLK):
        bias_b = nn(perm, bias[b * 64 : (b + 1) * 64, :])
        for i in range(ROWS):
            s = s_in[i, b] + bias_b
            e = jnp.exp(s - jnp.max(s, axis=-1, keepdims=True))
            p = (e * (1.0 / jnp.sum(e, axis=-1, keepdims=True))).astype(BF16)
            vb = jnp.concatenate(
                [v[i, pl.ds(pl.multiple_of(lists[b, t] * BLK, BLK), BLK), :] for t in range(2)], axis=0
            )
            o64 = nn(p, vb)
            o = o64[0:QB]
            for k in range(1, HEADS):
                o = jnp.where(lane16 == k, o64[k * QB : (k + 1) * QB], o)
            gated = jax.nn.sigmoid(gate[i, b * QB : (b + 1) * QB, :].astype(F32)) * o
            acc[pl.ds(b * 64 + i, QB, stride=4), :] = gated
    out[...] = nn(acc[...].astype(BF16), w_out[...]).astype(BF16)


def call(kernel, ins, outs, scratch=(), flops=0, nbytes=0):
    return pl.pallas_call(
        kernel,
        in_specs=ins,
        out_specs=[VMEM] * len(outs) if isinstance(outs, list) else VMEM,
        out_shape=outs,
        scratch_shapes=list(scratch),
        compiler_params=pltpu.CompilerParams(vmem_limit_bytes=LIMIT),
        cost_estimate=pl.CostEstimate(flops=flops, bytes_accessed=nbytes, transcendentals=0),
    )


def local(pair, w_query, w_key, w_value, w_gate, w_bias, w_out, shift, block_lists, chain_ids):
    shape = jax.ShapeDtypeStruct
    packed = call(pack_kernel, [VMEM] * 6 + [SMEM], shape((176, N), BF16), nbytes=400000)(
        pair.transpose(0, 2, 1), w_query.T, w_key.T, w_value.T, w_gate.T, w_bias.T, shift
    )
    g = lax.all_gather(packed, "head", axis=0)
    mine = call(bias_kernel, [SMEM, VMEM], shape((512, 128), BF16), nbytes=400000)(block_lists, g)
    bias = lax.all_to_all(mine.reshape(128, 4, 128), "row", 0, 0, tiled=True).reshape(512, 128)
    scores, v, gate = call(
        score_kernel,
        [SMEM, VMEM, VMEM],
        [shape((ROWS, NBLK, 64, 128), F32), shape((ROWS, N, 128), BF16), shape((ROWS, 128, 128), BF16)],
        [pltpu.VMEM((ROWS, N, 128), BF16)],
        flops=1000000000,
        nbytes=4000000,
    )(block_lists, chain_ids.reshape(1, N), g)
    mixed = call(
        mix_kernel,
        [SMEM] + [VMEM] * 5,
        shape((512, 128), BF16),
        [pltpu.VMEM((512, 128), F32)],
        flops=100000000,
        nbytes=3000000,
    )(block_lists, bias, scores, v, gate, w_out)
    moved = lax.all_to_all(mixed.reshape(128, 4, 128), "row", 0, 0, tiled=True)
    return moved.reshape(512, 1, 128)


def solution(mesh):
    in_specs = (
        P("row", None, "head"),
        P(None, "head"),
        P(None, "head"),
        P(None, "head"),
        P(None, "head"),
        P(None, "head"),
        P(),
        P("head"),
        P(),
        P(),
    )
    out_specs = P(None, ("row", "head"), None)
    return jax.shard_map(local, mesh=mesh, in_specs=in_specs, out_specs=out_specs, check_vma=False)
```

```python
import math

import jax
import jax.numpy as jnp
import numpy as np
from jax import lax
from jax.experimental import pallas as pl
from jax.experimental.pallas import tpu as pltpu
from jax.sharding import PartitionSpec as P

F32, BF16 = jnp.float32, jnp.bfloat16
VMEM = pl.BlockSpec(memory_space=pltpu.VMEM)
HBM = pl.BlockSpec(memory_space=pltpu.HBM)
LIMIT = 24 * 1024 * 1024
HEADS, HD, N = 4, 32, 512
DEVICES = np.arange(512).reshape(8, 16, 2, 2)
OVER_BLOCK = DEVICES.transpose(1, 3, 0, 2).reshape(32, 16).tolist()
OVER_Z = DEVICES.transpose(0, 3, 1, 2).reshape(16, 32).tolist()
OVER_CORE = [[0, 1], [2, 3]]
Q, I = 32, 16
MSG = 96


def nt(a, b):
    return lax.dot_general(a, b, (((1,), (1,)), ((), ())), preferred_element_type=F32)


def nn(a, b):
    return jnp.dot(a, b, preferred_element_type=F32)


def iota(shape, dim):
    return lax.broadcasted_iota(jnp.int32, shape, dim)


def place():
    row, head = lax.axis_index("row"), lax.axis_index("head")
    return row // 16, head // 2, head % 2, head


def pack_kernel(pair, wq, wk, wv, wg, wb, chain, lists, shift, out, same_out, sel_out, x, w, wb_v, chain_v, halves, sem):
    b, _, core, head = place()
    copies = [
        pltpu.make_async_copy(pair, x, sem.at[0]),
        pltpu.make_async_copy(wq, w.at[0:32], sem.at[1]),
        pltpu.make_async_copy(wk, w.at[32:64], sem.at[2]),
        pltpu.make_async_copy(wv, w.at[64:96], sem.at[3]),
        pltpu.make_async_copy(wg, w.at[96:128], sem.at[4]),
        pltpu.make_async_copy(wb, wb_v, sem.at[5]),
        pltpu.make_async_copy(chain, chain_v, sem.at[6]),
    ]
    for copy in copies:
        copy.start()
    for copy in copies:
        copy.wait()
    s = jnp.full((16, 128), shift[0], F32)
    hi = s.astype(BF16).astype(F32)
    mid = (s - hi).astype(BF16).astype(F32)
    low = s - hi - mid
    wide = jnp.broadcast_to(wb_v[...].astype(F32), (16, 128))
    row = iota((16, 128), 0)
    part = row // 4
    small = jnp.where(part == 0, wide, jnp.where(part == 1, hi, jnp.where(part == 2, mid, low)))
    small = jnp.where(row % 4 == head, small, 0.0).astype(BF16)
    w_part = w[pl.ds(pl.multiple_of(b * 16, 16), 16), :]
    flat = x[...].reshape(128, N)
    halves[0] = flat
    for c in range(4):
        halves[1, :, c * 128 : (c + 1) * 128] = pltpu.roll(flat[:, c * 128 : (c + 1) * 128].astype(F32), 64, 1).astype(BF16)
    lane = iota((128, 128), 1)
    for d in range(8):
        b0, b1 = lists[0, d], lists[1, d]
        first = halves[b0 % 2, :, pl.ds(pl.multiple_of(b0 // 2 * 128, 128), 128)]
        second = halves[1 - b1 % 2, :, pl.ds(pl.multiple_of(b1 // 2 * 128, 128), 128)]
        keys = jnp.where(lane < 64, first, second)
        for y in range(2):
            at = (2 * d + y) * MSG
            out[at : at + 64] = keys[y * 64 : (y + 1) * 64]
            out[at + 64 : at + 80] = w_part
            out[at + 80 : at + 96] = small
    b0, b1 = lists[0, b], lists[1, b]
    c0 = jnp.broadcast_to(chain_v[:, pl.ds(pl.multiple_of(b0 // 2 * 128, 128), 128)].astype(F32), (Q, 128))
    c1 = jnp.broadcast_to(chain_v[:, pl.ds(pl.multiple_of(b1 // 2 * 128, 128), 128)].astype(F32), (Q, 128))
    c0 = jnp.where(b0 % 2 == 0, c0, pltpu.roll(c0, 64, 1))
    c1 = jnp.where(b1 % 2 == 1, c1, pltpu.roll(c1, 64, 1))
    key_chain = jnp.where(iota((Q, 128), 1) < 64, c0, c1)
    own = jnp.where(b0 == b, 0, 64)
    sel = iota((Q, 128), 1) == own + 2 * iota((Q, 128), 0) + core
    query_chain = jnp.sum(jnp.where(sel, key_chain, 0.0), axis=-1, keepdims=True)
    same_out[...] = (query_chain == key_chain).astype(F32)
    sel_out[...] = sel.astype(BF16)


def heads_small(g):
    return sum(g[c, y, 80:96, :].astype(F32) for c in range(2) for y in range(2))


def bias_kernel(g, out):
    b, _, core, _ = place()
    z = jnp.concatenate(
        [g[k % 2, 2 * b + k // 2, pl.ds(pl.multiple_of(core * 32, 32), 32), :] for k in range(HEADS)], axis=0
    )
    found = nn(heads_small(g).astype(BF16), z)[0:4]
    tile = jnp.concatenate([found] * 4, axis=0).astype(BF16)
    for r in range(8):
        out[r * 16 : (r + 1) * 16, :] = tile


def score_kernel(g, same, sel, s_out, v_out, gate_out, zq_scr, k_scr):
    small = heads_small(g)
    scale = 1.0 / math.sqrt(HD)
    selector = sel[...]
    w = [
        jnp.concatenate([g[k % 2, 2 * s + k // 2, 64:80, :] for k in range(HEADS) for s in (2 * t, 2 * t + 1)], axis=0)
        for t in range(4)
    ]
    w_kv = jnp.concatenate([w[1], w[2]], axis=0)
    w_qg = jnp.concatenate([w[0], w[3]], axis=0)
    for i in range(I):
        s, t = i // 2, i % 2
        zt = jnp.concatenate([g[k % 2, 2 * s + k // 2, t * 32 : (t + 1) * 32, :] for k in range(HEADS)], axis=0)
        kv = nn(w_kv, zt).astype(BF16)
        k_scr[i] = kv[0:128]
        v_out[i] = kv[128:256]
        zq_scr[i * Q : (i + 1) * Q] = nt(selector, zt).astype(BF16)
    qg = nt(zq_scr[...], w_qg).astype(BF16)
    gate_out[...] = qg[:, 128:256]
    head_of_lane = iota((Q, 128), 1) // HD
    moved = jnp.concatenate(
        [same[...] * (small[4 + k : 5 + k] + small[8 + k : 9 + k] + small[12 + k : 13 + k]) for k in range(HEADS)], axis=0
    )
    for i in range(I):
        q = qg[i * Q : (i + 1) * Q, 0:128]
        zero = jnp.zeros_like(q)
        q_all = jnp.concatenate([jnp.where(head_of_lane == k, q, zero) for k in range(HEADS)], axis=0)
        s_out[i] = nn(q_all, k_scr[i]) * scale + moved


def mix_kernel(bias, s_in, v, gate, w_out, out, acc):
    perm = (iota((128, 128), 1) == (iota((128, 128), 0) % Q) * 4 + iota((128, 128), 0) // Q).astype(BF16)
    head_of_lane = iota((Q, 128), 1) // HD
    plane = nn(perm, bias[...])
    for i in range(I):
        s = s_in[i] + plane
        e = jnp.exp(s - jnp.max(s, axis=-1, keepdims=True))
        p = (e * (1.0 / jnp.sum(e, axis=-1, keepdims=True))).astype(BF16)
        every = nt(p, v[i])
        o = every[0:Q]
        for k in range(1, HEADS):
            o = jnp.where(head_of_lane == k, every[k * Q : (k + 1) * Q], o)
        acc[pl.ds(i, Q, stride=I), :] = jax.nn.sigmoid(gate[i * Q : (i + 1) * Q, :].astype(F32)) * o
    out[...] = nn(acc[...].astype(BF16), w_out[...]).astype(BF16)


def order_kernel(moved, out, before, after):
    before[...] = moved[...].astype(F32)
    for s in range(8):
        for t in range(2):
            after[pl.ds(s * 64 + t, 32, stride=2), :] = before[pl.ds(2 * s + t, 32, stride=16), :]
    out[...] = after[...].astype(BF16)


def call(kernel, ins, outs, scratch=(), flops=0, nbytes=0, limit=LIMIT):
    return pl.pallas_call(
        kernel,
        in_specs=ins,
        out_specs=[VMEM] * len(outs) if isinstance(outs, list) else VMEM,
        out_shape=outs,
        scratch_shapes=list(scratch),
        compiler_params=pltpu.CompilerParams(vmem_limit_bytes=limit),
        cost_estimate=pl.CostEstimate(flops=flops, bytes_accessed=nbytes, transcendentals=0),
    )


def local(pair, w_query, w_key, w_value, w_gate, w_bias, w_out, shift, block_lists, chain_ids):
    shape = jax.ShapeDtypeStruct
    smem = pl.BlockSpec(memory_space=pltpu.SMEM)
    packed, same, sel = call(
        pack_kernel,
        [HBM] * 7 + [smem] * 2,
        [shape((16 * MSG, 128), BF16), shape((Q, 128), F32), shape((Q, 128), BF16)],
        [
            pltpu.VMEM((4, 32, N), BF16),
            pltpu.VMEM((128, 128), BF16),
            pltpu.VMEM((1, 128), BF16),
            pltpu.VMEM((1, N), jnp.int32),
            pltpu.VMEM((2, 128, N), BF16),
            pltpu.SemaphoreType.DMA((7,)),
        ],
        nbytes=1000000,
        limit=None,
    )(
        pair.transpose(0, 2, 1), w_query.T, w_key.T, w_value.T, w_gate.T, w_bias.T,
        chain_ids.reshape(1, N), block_lists.T, shift,
    )
    got = lax.all_to_all(
        packed.reshape(16, MSG, 128), ("row", "head"), 0, 0, tiled=True, axis_index_groups=OVER_BLOCK
    )
    g = lax.all_gather(got, "head", axis=0, axis_index_groups=OVER_CORE)
    mine = call(bias_kernel, [VMEM], shape((128, 128), BF16), nbytes=400000)(g)
    bias = lax.all_to_all(
        mine.reshape(32, 4, 128), ("row", "head"), 0, 0, tiled=True, axis_index_groups=OVER_Z
    ).reshape(128, 128)
    scores, v, gate = call(
        score_kernel,
        [VMEM] * 3,
        [shape((I, 128, 128), F32), shape((I, 128, 128), BF16), shape((I * Q, 128), BF16)],
        [pltpu.VMEM((I * Q, 128), BF16), pltpu.VMEM((I, 128, 128), BF16)],
        flops=1000000000,
        nbytes=4000000,
    )(g, same, sel)
    mixed = call(
        mix_kernel,
        [VMEM] * 5,
        shape((I * Q, 128), BF16),
        [pltpu.VMEM((I * Q, 128), F32)],
        flops=100000000,
        nbytes=3000000,
    )(bias, scores, v, gate, w_out)
    moved = lax.all_to_all(
        mixed.reshape(32, I, 128), ("row", "head"), 0, 0, tiled=True, axis_index_groups=OVER_Z
    ).reshape(512, 128)
    ordered = call(
        order_kernel, [VMEM], shape((512, 128), BF16), [pltpu.VMEM((512, 128), F32)] * 2, nbytes=300000
    )(moved)
    return ordered.reshape(512, 1, 128)


def solution(mesh):
    in_specs = (
        P("row", None, "head"),
        P(None, "head"),
        P(None, "head"),
        P(None, "head"),
        P(None, "head"),
        P(None, "head"),
        P(),
        P("head"),
        P(),
        P(),
    )
    out_specs = P(None, ("row", "head"), None)
    return jax.shard_map(local, mesh=mesh, in_specs=in_specs, out_specs=out_specs, check_vma=False)
```

```python
import math

import jax
import jax.numpy as jnp
import numpy as np
from jax import lax
from jax.experimental import pallas as pl
from jax.experimental.pallas import tpu as pltpu
from jax.sharding import PartitionSpec as P

F32, BF16 = jnp.float32, jnp.bfloat16
VMEM = pl.BlockSpec(memory_space=pltpu.VMEM)
HBM = pl.BlockSpec(memory_space=pltpu.HBM)
LIMIT = 24 * 1024 * 1024
HEADS, HD, N = 4, 32, 512
DEVICES = np.arange(512).reshape(8, 16, 2, 2)
FAR = 6
OVER_BLOCK = DEVICES[np.arange(8) ^ FAR].transpose(1, 3, 0, 2).reshape(32, 16).tolist()
TURN_BIAS, TURN_OUT = 8, 8
OVER_Z_BIAS = np.roll(DEVICES, -TURN_BIAS, 1).transpose(0, 3, 1, 2).reshape(16, 32).tolist()
OVER_Z_OUT = np.roll(DEVICES, -TURN_OUT, 1).transpose(0, 3, 1, 2).reshape(16, 32).tolist()
OVER_CORE = [[0, 1], [2, 3]]
Q, I = 32, 16
MSG = 96


def nt(a, b):
    return lax.dot_general(a, b, (((1,), (1,)), ((), ())), preferred_element_type=F32)


def nn(a, b):
    return jnp.dot(a, b, preferred_element_type=F32)


def iota(shape, dim):
    return lax.broadcasted_iota(jnp.int32, shape, dim)


def place():
    row, head = lax.axis_index("row"), lax.axis_index("head")
    return row // 16, head // 2, head % 2, head


def pack_kernel(
    pair, wq, wk, wv, wg, wb, chain, lists_in, shift_in,
    out, same_out, sel_out,
    x, w, wb_v, chain_v, lists, shift, halves, message, same_v, sel_v, sem,
):
    b, _, core, head = place()
    copies = [
        pltpu.make_async_copy(lists_in, lists, sem.at[0]),
        pltpu.make_async_copy(chain, chain_v, sem.at[1]),
        pltpu.make_async_copy(shift_in, shift, sem.at[2]),
        pltpu.make_async_copy(wb, wb_v, sem.at[3]),
        pltpu.make_async_copy(pair, x, sem.at[4]),
        pltpu.make_async_copy(wq, w.at[0:32], sem.at[5]),
        pltpu.make_async_copy(wk, w.at[32:64], sem.at[6]),
        pltpu.make_async_copy(wv, w.at[64:96], sem.at[7]),
        pltpu.make_async_copy(wg, w.at[96:128], sem.at[8]),
    ]
    for copy in copies:
        copy.start()
    copies[0].wait()
    copies[1].wait()
    b0, b1 = lists[0, b], lists[1, b]
    c0 = jnp.broadcast_to(chain_v[:, pl.ds(pl.multiple_of(b0 // 2 * 128, 128), 128)].astype(F32), (Q, 128))
    c1 = jnp.broadcast_to(chain_v[:, pl.ds(pl.multiple_of(b1 // 2 * 128, 128), 128)].astype(F32), (Q, 128))
    c0 = jnp.where(b0 % 2 == 0, c0, pltpu.roll(c0, 64, 1))
    c1 = jnp.where(b1 % 2 == 1, c1, pltpu.roll(c1, 64, 1))
    key_chain = jnp.where(iota((Q, 128), 1) < 64, c0, c1)
    own = jnp.where(b0 == b, 0, 64)
    sel = iota((Q, 128), 1) == own + (2 * iota((Q, 128), 0) + 4 * TURN_OUT) % 64 + core
    query_chain = jnp.sum(jnp.where(sel, key_chain, 0.0), axis=-1, keepdims=True)
    same_v[...] = (query_chain == key_chain).astype(F32)
    sel_v[...] = sel.astype(BF16)
    sent = [
        pltpu.make_async_copy(same_v, same_out, sem.at[9]),
        pltpu.make_async_copy(sel_v, sel_out, sem.at[10]),
    ]
    for copy in sent:
        copy.start()
    for copy in copies[2:]:
        copy.wait()
    s = jnp.broadcast_to(shift[...], (16, 128))
    hi = s.astype(BF16).astype(F32)
    mid = (s - hi).astype(BF16).astype(F32)
    low = s - hi - mid
    wide = jnp.broadcast_to(wb_v[...].astype(F32), (16, 128))
    row = iota((16, 128), 0)
    part = row // 4
    small = jnp.where(part == 0, wide, jnp.where(part == 1, hi, jnp.where(part == 2, mid, low)))
    small = jnp.where(row % 4 == head, small, 0.0).astype(BF16)
    w_part = w[pl.ds(pl.multiple_of(b * 16, 16), 16), :]
    flat = x[...].reshape(128, N)
    halves[0] = flat
    for c in range(4):
        halves[1, :, c * 128 : (c + 1) * 128] = pltpu.roll(flat[:, c * 128 : (c + 1) * 128].astype(F32), 64, 1).astype(BF16)
    lane = iota((128, 128), 1)
    for d in range(8):
        b0, b1 = lists[0, d], lists[1, d]
        first = halves[b0 % 2, :, pl.ds(pl.multiple_of(b0 // 2 * 128, 128), 128)]
        second = halves[1 - b1 % 2, :, pl.ds(pl.multiple_of(b1 // 2 * 128, 128), 128)]
        keys = jnp.where(lane < 64, first, second)
        start = 2 * (d ^ FAR) * MSG
        for y in range(2):
            at = start + y * MSG
            message[at : at + 64] = keys[y * 64 : (y + 1) * 64]
            message[at + 64 : at + 80] = w_part
            message[at + 80 : at + 96] = small
        span = pl.ds(start, 2 * MSG)
        sent.append(pltpu.make_async_copy(message.at[span], out.at[span], sem.at[11 + d]))
        sent[-1].start()
    for copy in sent:
        copy.wait()


def heads_small(g):
    return sum(g[c, y, 80:96, :].astype(F32) for c in range(2) for y in range(2))


def bias_kernel(g, out):
    b, _, core, _ = place()
    z = jnp.concatenate(
        [g[k % 2, 2 * (b ^ FAR) + k // 2, pl.ds(pl.multiple_of(core * 32, 32), 32), :] for k in range(HEADS)], axis=0
    )
    found = nn(heads_small(g).astype(BF16), z)[0:4]
    tile = jnp.concatenate([found] * 4, axis=0).astype(BF16)
    for r in range(8):
        out[r * 16 : (r + 1) * 16, :] = tile


def score_kernel(g, same, sel, s_out, v_out, gate_out, zq_scr, k_scr):
    small = heads_small(g)
    scale = 1.0 / math.sqrt(HD)
    selector = sel[...]
    w = [
        jnp.concatenate([g[k % 2, 2 * (s ^ FAR) + k // 2, 64:80, :] for k in range(HEADS) for s in (2 * t, 2 * t + 1)], axis=0)
        for t in range(4)
    ]
    w_kv = jnp.concatenate([w[1], w[2]], axis=0)
    w_qg = jnp.concatenate([w[0], w[3]], axis=0)
    for i in range(I):
        s, t = i // 2, i % 2
        zt = jnp.concatenate([g[k % 2, 2 * (s ^ FAR) + k // 2, t * 32 : (t + 1) * 32, :] for k in range(HEADS)], axis=0)
        kv = nn(w_kv, zt).astype(BF16)
        k_scr[i] = kv[0:128]
        v_out[i] = kv[128:256]
        zq_scr[i * Q : (i + 1) * Q] = nt(selector, zt).astype(BF16)
    qg = nt(zq_scr[...], w_qg).astype(BF16)
    gate_out[...] = qg[:, 128:256]
    head_of_lane = iota((Q, 128), 1) // HD
    moved = jnp.concatenate(
        [same[...] * (small[4 + k : 5 + k] + small[8 + k : 9 + k] + small[12 + k : 13 + k]) for k in range(HEADS)], axis=0
    )
    for i in range(I):
        q = qg[i * Q : (i + 1) * Q, 0:128]
        zero = jnp.zeros_like(q)
        q_all = jnp.concatenate([jnp.where(head_of_lane == k, q, zero) for k in range(HEADS)], axis=0)
        s_out[i] = nn(q_all, k_scr[i]) * scale + moved


def mix_kernel(bias, s_in, v, gate, w_out, out, acc):
    row = iota((128, 128), 0)
    peer = (row % Q + 2 * (TURN_OUT - TURN_BIAS)) % Q
    perm = (iota((128, 128), 1) == peer * 4 + row // Q).astype(BF16)
    head_of_lane = iota((Q, 128), 1) // HD
    plane = nn(perm, bias[...])
    for i in range(I):
        s = s_in[i] + plane
        e = jnp.exp(s - jnp.max(s, axis=-1, keepdims=True))
        p = (e * (1.0 / jnp.sum(e, axis=-1, keepdims=True))).astype(BF16)
        every = nt(p, v[i])
        o = every[0:Q]
        for k in range(1, HEADS):
            o = jnp.where(head_of_lane == k, every[k * Q : (k + 1) * Q], o)
        acc[pl.ds(i, Q, stride=I), :] = jax.nn.sigmoid(gate[i * Q : (i + 1) * Q, :].astype(F32)) * o
    out[...] = nn(acc[...].astype(BF16), w_out[...]).astype(BF16)


def order_kernel(moved, out, before, after):
    before[...] = moved[...].astype(F32)
    for s in range(8):
        for t in range(2):
            n = 2 * TURN_OUT
            after[pl.ds(s * 64 + 2 * n + t, 32 - n, stride=2), :] = before[pl.ds(2 * s + t, 32 - n, stride=16), :]
            after[pl.ds(s * 64 + t, n, stride=2), :] = before[pl.ds((32 - n) * 16 + 2 * s + t, n, stride=16), :]
    out[...] = after[...].astype(BF16)


def call(kernel, ins, outs, scratch=(), flops=0, nbytes=0):
    return pl.pallas_call(
        kernel,
        in_specs=ins,
        out_specs=[VMEM] * len(outs) if isinstance(outs, list) else VMEM,
        out_shape=outs,
        scratch_shapes=list(scratch),
        compiler_params=pltpu.CompilerParams(vmem_limit_bytes=LIMIT),
        cost_estimate=pl.CostEstimate(flops=flops, bytes_accessed=nbytes, transcendentals=0),
    )


def local(pair, w_query, w_key, w_value, w_gate, w_bias, w_out, shift, block_lists, chain_ids):
    shape = jax.ShapeDtypeStruct
    packed, same, sel = pl.pallas_call(
        pack_kernel,
        in_specs=[HBM] * 9,
        out_specs=[HBM] * 3,
        out_shape=[shape((16 * MSG, 128), BF16), shape((Q, 128), F32), shape((Q, 128), BF16)],
        scratch_shapes=[
            pltpu.VMEM((4, 32, N), BF16),
            pltpu.VMEM((128, 128), BF16),
            pltpu.VMEM((1, 128), BF16),
            pltpu.VMEM((1, N), jnp.int32),
            pltpu.SMEM((2, 8), jnp.int32),
            pltpu.VMEM((1, 1), F32),
            pltpu.VMEM((2, 128, N), BF16),
            pltpu.VMEM((16 * MSG, 128), BF16),
            pltpu.VMEM((Q, 128), F32),
            pltpu.VMEM((Q, 128), BF16),
            pltpu.SemaphoreType.DMA((19,)),
        ],
        cost_estimate=pl.CostEstimate(flops=0, bytes_accessed=1000000, transcendentals=0),
    )(
        pair.transpose(0, 2, 1), w_query.T, w_key.T, w_value.T, w_gate.T, w_bias.T,
        chain_ids.reshape(1, N), block_lists.T, shift.reshape(1, 1),
    )
    got = lax.all_to_all(
        packed.reshape(16, MSG, 128), ("row", "head"), 0, 0, tiled=True, axis_index_groups=OVER_BLOCK
    )
    g = lax.all_gather(got, "head", axis=0, axis_index_groups=OVER_CORE)
    mine = call(bias_kernel, [VMEM], shape((128, 128), BF16), nbytes=400000)(g)
    bias = lax.all_to_all(
        mine.reshape(32, 4, 128), ("row", "head"), 0, 0, tiled=True, axis_index_groups=OVER_Z_BIAS
    ).reshape(128, 128)
    scores, v, gate = call(
        score_kernel,
        [VMEM] * 3,
        [shape((I, 128, 128), F32), shape((I, 128, 128), BF16), shape((I * Q, 128), BF16)],
        [pltpu.VMEM((I * Q, 128), BF16), pltpu.VMEM((I, 128, 128), BF16)],
        flops=1000000000,
        nbytes=4000000,
    )(g, same, sel)
    mixed = call(
        mix_kernel,
        [VMEM] * 5,
        shape((I * Q, 128), BF16),
        [pltpu.VMEM((I * Q, 128), F32)],
        flops=100000000,
        nbytes=3000000,
    )(bias, scores, v, gate, w_out)
    moved = lax.all_to_all(
        mixed.reshape(32, I, 128), ("row", "head"), 0, 0, tiled=True, axis_index_groups=OVER_Z_OUT
    ).reshape(512, 128)
    ordered = call(
        order_kernel, [VMEM], shape((512, 128), BF16), [pltpu.VMEM((512, 128), F32)] * 2, nbytes=300000
    )(moved)
    return ordered.reshape(512, 1, 128)


def solution(mesh):
    in_specs = (
        P("row", None, "head"),
        P(None, "head"),
        P(None, "head"),
        P(None, "head"),
        P(None, "head"),
        P(None, "head"),
        P(),
        P("head"),
        P(),
        P(),
    )
    out_specs = P(None, ("row", "head"), None)
    return jax.shard_map(local, mesh=mesh, in_specs=in_specs, out_specs=out_specs, check_vma=False)
```

```python
import math

import jax
import jax.numpy as jnp
import numpy as np
from jax import lax
from jax.experimental import pallas as pl
from jax.experimental.pallas import tpu as pltpu
from jax.sharding import PartitionSpec as P

F32, BF16 = jnp.float32, jnp.bfloat16
VMEM = pl.BlockSpec(memory_space=pltpu.VMEM)
HBM = pl.BlockSpec(memory_space=pltpu.HBM)
LIMIT = 24 * 1024 * 1024
HEADS, HD, N = 4, 32, 512
DEVICES = np.arange(512).reshape(8, 16, 2, 2)
FAR = [0] + [6] * 15
OVER_BLOCK = [
    group
    for z in range(16)
    for group in DEVICES[np.arange(8) ^ FAR[z], z].transpose(2, 0, 1).reshape(2, 16).tolist()
]
FIRST_BIAS, FIRST_OUT, STEP = 9, 8, 1
BACK = pow(STEP, -1, 16)


def along_z(first):
    return DEVICES[:, (first + STEP * np.arange(16)) % 16].transpose(0, 3, 1, 2).reshape(16, 32).tolist()


OVER_CORE = [[0, 1], [2, 3]]
Q, I = 32, 16
MSG = 80
NEAR = 144


def nt(a, b):
    return lax.dot_general(a, b, (((1,), (1,)), ((), ())), preferred_element_type=F32)


def nn(a, b):
    return jnp.dot(a, b, preferred_element_type=F32)


def iota(shape, dim):
    return lax.broadcasted_iota(jnp.int32, shape, dim)


def place():
    row, head = lax.axis_index("row"), lax.axis_index("head")
    return row // 16, head // 2, head % 2, head


def far():
    return jnp.where(lax.axis_index("row") % 16 == 0, FAR[0], FAR[1])


def pack_kernel(
    pair, wq, wk, wv, wg, wb, chain, lists_in, shift_in,
    out, near_out, same_out, sel_out,
    x, w, wb_v, chain_v, lists, shift, halves, message, near, same_v, sel_v, sem,
):
    b, _, core, head = place()
    copies = [
        pltpu.make_async_copy(lists_in, lists, sem.at[0]),
        pltpu.make_async_copy(chain, chain_v, sem.at[1]),
        pltpu.make_async_copy(shift_in, shift, sem.at[2]),
        pltpu.make_async_copy(wb, wb_v, sem.at[3]),
        pltpu.make_async_copy(pair, x, sem.at[4]),
        pltpu.make_async_copy(wq, w.at[0:32], sem.at[5]),
        pltpu.make_async_copy(wk, w.at[32:64], sem.at[6]),
        pltpu.make_async_copy(wv, w.at[64:96], sem.at[7]),
        pltpu.make_async_copy(wg, w.at[96:128], sem.at[8]),
    ]
    for copy in copies:
        copy.start()
    copies[0].wait()
    copies[1].wait()
    b0, b1 = lists[0, b], lists[1, b]
    c0 = jnp.broadcast_to(chain_v[:, pl.ds(pl.multiple_of(b0 // 2 * 128, 128), 128)].astype(F32), (Q, 128))
    c1 = jnp.broadcast_to(chain_v[:, pl.ds(pl.multiple_of(b1 // 2 * 128, 128), 128)].astype(F32), (Q, 128))
    c0 = jnp.where(b0 % 2 == 0, c0, pltpu.roll(c0, 64, 1))
    c1 = jnp.where(b1 % 2 == 1, c1, pltpu.roll(c1, 64, 1))
    key_chain = jnp.where(iota((Q, 128), 1) < 64, c0, c1)
    own = jnp.where(b0 == b, 0, 64)
    p = iota((Q, 128), 0)
    sel = iota((Q, 128), 1) == own + (FIRST_OUT + STEP * (p // 2)) % 16 * 4 + p % 2 * 2 + core
    query_chain = jnp.sum(jnp.where(sel, key_chain, 0.0), axis=-1, keepdims=True)
    same_v[...] = (query_chain == key_chain).astype(F32)
    sel_v[...] = sel.astype(BF16)
    sent = [
        pltpu.make_async_copy(same_v, same_out, sem.at[9]),
        pltpu.make_async_copy(sel_v, sel_out, sem.at[10]),
    ]
    for copy in sent:
        copy.start()
    for copy in copies[2:]:
        copy.wait()
    s = jnp.broadcast_to(shift[...], (16, 128))
    hi = s.astype(BF16).astype(F32)
    mid = (s - hi).astype(BF16).astype(F32)
    low = s - hi - mid
    wide = jnp.broadcast_to(wb_v[...].astype(F32), (16, 128))
    row = iota((16, 128), 0)
    part = row // 4
    small = jnp.where(part == 0, wide, jnp.where(part == 1, hi, jnp.where(part == 2, mid, low)))
    small = jnp.where(row % 4 == head, small, 0.0).astype(BF16)
    w_part = w[pl.ds(pl.multiple_of(b * 16, 16), 16), :]
    flat = x[...].reshape(128, N)
    halves[0] = flat
    for c in range(4):
        halves[1, :, c * 128 : (c + 1) * 128] = pltpu.roll(flat[:, c * 128 : (c + 1) * 128].astype(F32), 64, 1).astype(BF16)
    lane = iota((128, 128), 1)

    def listed(d):
        b0, b1 = lists[0, d], lists[1, d]
        first = halves[b0 % 2, :, pl.ds(pl.multiple_of(b0 // 2 * 128, 128), 128)]
        second = halves[1 - b1 % 2, :, pl.ds(pl.multiple_of(b1 // 2 * 128, 128), 128)]
        return jnp.where(lane < 64, first, second)

    away = far()
    for n in range(8):
        keys = listed(n ^ away)
        start = 2 * n * MSG
        for y in range(2):
            at = start + y * MSG
            message[at : at + 64] = keys[y * 64 : (y + 1) * 64]
            message[at + 64 : at + 80] = w_part
        span = pl.ds(start, 2 * MSG)
        sent.append(pltpu.make_async_copy(message.at[span], out.at[span], sem.at[11 + n]))
        sent[-1].start()
    near[0:128] = listed(b)
    near[128:144] = small
    sent.append(pltpu.make_async_copy(near, near_out, sem.at[19]))
    sent[-1].start()
    for copy in sent:
        copy.wait()


def heads_small(near):
    return sum(near[k, 128:144, :].astype(F32) for k in range(HEADS))


def bias_kernel(near, out):
    rows = pl.ds(pl.multiple_of(place()[3] * 32, 32), 32)
    z = jnp.concatenate([near[k, rows, :] for k in range(HEADS)], axis=0)
    found = nn(heads_small(near).astype(BF16), z)[0:4]
    tile = jnp.concatenate([found] * 4, axis=0).astype(BF16)
    for r in range(8):
        out[r * 16 : (r + 1) * 16, :] = tile


def score_kernel(g, near, same, sel, s_out, v_out, gate_out, zq_scr, k_scr):
    small = heads_small(near)
    scale = 1.0 / math.sqrt(HD)
    selector = sel[...]
    away = far()
    w = [
        jnp.concatenate([g[k % 2, 2 * (s ^ away) + k // 2, 64:80, :] for k in range(HEADS) for s in (2 * t, 2 * t + 1)], axis=0)
        for t in range(4)
    ]
    w_kv = jnp.concatenate([w[1], w[2]], axis=0)
    w_qg = jnp.concatenate([w[0], w[3]], axis=0)
    for i in range(I):
        s, t = i // 2, i % 2
        zt = jnp.concatenate([g[k % 2, 2 * s + k // 2, t * 32 : (t + 1) * 32, :] for k in range(HEADS)], axis=0)
        kv = nn(w_kv, zt).astype(BF16)
        k_scr[i] = kv[0:128]
        v_out[i] = kv[128:256]
        zq_scr[i * Q : (i + 1) * Q] = nt(selector, zt).astype(BF16)
    qg = nt(zq_scr[...], w_qg).astype(BF16)
    gate_out[...] = qg[:, 128:256]
    head_of_lane = iota((Q, 128), 1) // HD
    moved = jnp.concatenate(
        [same[...] * (small[4 + k : 5 + k] + small[8 + k : 9 + k] + small[12 + k : 13 + k]) for k in range(HEADS)], axis=0
    )
    for i in range(I):
        q = qg[i * Q : (i + 1) * Q, 0:128]
        zero = jnp.zeros_like(q)
        q_all = jnp.concatenate([jnp.where(head_of_lane == k, q, zero) for k in range(HEADS)], axis=0)
        s_out[i] = nn(q_all, k_scr[i]) * scale + moved


def mix_kernel(bias, s_in, v, gate, w_out, out, acc):
    row = iota((128, 128), 0)
    n = (row % Q // 2 + BACK * (FIRST_OUT - FIRST_BIAS + 16)) % 16
    perm = (iota((128, 128), 1) == (2 * n + row % 2) * 4 + row // Q).astype(BF16)
    head_of_lane = iota((Q, 128), 1) // HD
    plane = nn(perm, bias[...])
    away = far()
    for i in range(I):
        s = s_in[i] + plane
        e = jnp.exp(s - jnp.max(s, axis=-1, keepdims=True))
        p = (e * (1.0 / jnp.sum(e, axis=-1, keepdims=True))).astype(BF16)
        every = nt(p, v[i])
        o = every[0:Q]
        for k in range(1, HEADS):
            o = jnp.where(head_of_lane == k, every[k * Q : (k + 1) * Q], o)
        acc[pl.ds((i // 2 ^ away) * 2 + i % 2, Q, stride=I), :] = jax.nn.sigmoid(gate[i * Q : (i + 1) * Q, :].astype(F32)) * o
    out[...] = nn(acc[...].astype(BF16), w_out[...]).astype(BF16)


def order_kernel(moved, out, before, after):
    before[...] = moved[...].astype(F32)
    for p in range(32):
        z = (FIRST_OUT + STEP * (p // 2)) % 16
        for t in range(2):
            after[pl.ds(4 * z + 2 * (p % 2) + t, 8, stride=64), :] = before[pl.ds(p * 16 + t, 8, stride=2), :]
    out[...] = after[...].astype(BF16)


def call(kernel, ins, outs, scratch=(), flops=0, nbytes=0):
    return pl.pallas_call(
        kernel,
        in_specs=ins,
        out_specs=[VMEM] * len(outs) if isinstance(outs, list) else VMEM,
        out_shape=outs,
        scratch_shapes=list(scratch),
        compiler_params=pltpu.CompilerParams(vmem_limit_bytes=LIMIT),
        cost_estimate=pl.CostEstimate(flops=flops, bytes_accessed=nbytes, transcendentals=0),
    )


def local(pair, w_query, w_key, w_value, w_gate, w_bias, w_out, shift, block_lists, chain_ids):
    shape = jax.ShapeDtypeStruct
    packed, near, same, sel = pl.pallas_call(
        pack_kernel,
        in_specs=[HBM] * 9,
        out_specs=[HBM] * 4,
        out_shape=[shape((16 * MSG, 128), BF16), shape((NEAR, 128), BF16), shape((Q, 128), F32), shape((Q, 128), BF16)],
        scratch_shapes=[
            pltpu.VMEM((4, 32, N), BF16),
            pltpu.VMEM((128, 128), BF16),
            pltpu.VMEM((1, 128), BF16),
            pltpu.VMEM((1, N), jnp.int32),
            pltpu.SMEM((2, 8), jnp.int32),
            pltpu.VMEM((1, 1), F32),
            pltpu.VMEM((2, 128, N), BF16),
            pltpu.VMEM((16 * MSG, 128), BF16),
            pltpu.VMEM((NEAR, 128), BF16),
            pltpu.VMEM((Q, 128), F32),
            pltpu.VMEM((Q, 128), BF16),
            pltpu.SemaphoreType.DMA((20,)),
        ],
        cost_estimate=pl.CostEstimate(flops=0, bytes_accessed=1000000, transcendentals=0),
    )(
        pair.transpose(0, 2, 1), w_query.T, w_key.T, w_value.T, w_gate.T, w_bias.T,
        chain_ids.reshape(1, N), block_lists.T, shift.reshape(1, 1),
    )
    got = lax.all_to_all(
        packed.reshape(16, MSG, 128), ("row", "head"), 0, 0, tiled=True, axis_index_groups=OVER_BLOCK
    )
    g = lax.all_gather(got, "head", axis=0, axis_index_groups=OVER_CORE)
    near = lax.all_gather(near, "head", axis=0)
    mine = call(bias_kernel, [VMEM], shape((128, 128), BF16), nbytes=400000)(near)
    bias = lax.all_to_all(
        mine.reshape(32, 4, 128), ("row", "head"), 0, 0, tiled=True, axis_index_groups=along_z(FIRST_BIAS)
    ).reshape(128, 128)
    scores, v, gate = call(
        score_kernel,
        [VMEM] * 4,
        [shape((I, 128, 128), F32), shape((I, 128, 128), BF16), shape((I * Q, 128), BF16)],
        [pltpu.VMEM((I * Q, 128), BF16), pltpu.VMEM((I, 128, 128), BF16)],
        flops=1000000000,
        nbytes=4000000,
    )(g, near, same, sel)
    mixed = call(
        mix_kernel,
        [VMEM] * 5,
        shape((I * Q, 128), BF16),
        [pltpu.VMEM((I * Q, 128), F32)],
        flops=100000000,
        nbytes=3000000,
    )(bias, scores, v, gate, w_out)
    moved = lax.all_to_all(
        mixed.reshape(32, I, 128), ("row", "head"), 0, 0, tiled=True, axis_index_groups=along_z(FIRST_OUT)
    ).reshape(512, 128)
    ordered = call(
        order_kernel, [VMEM], shape((512, 128), BF16), [pltpu.VMEM((512, 128), F32)] * 2, nbytes=300000
    )(moved)
    return ordered.reshape(512, 1, 128)


def solution(mesh):
    in_specs = (
        P("row", None, "head"),
        P(None, "head"),
        P(None, "head"),
        P(None, "head"),
        P(None, "head"),
        P(None, "head"),
        P(),
        P("head"),
        P(),
        P(),
    )
    out_specs = P(None, ("row", "head"), None)
    return jax.shard_map(local, mesh=mesh, in_specs=in_specs, out_specs=out_specs, check_vma=False)
```

```python
import math

import jax
import jax.numpy as jnp
import numpy as np
from jax import lax
from jax.experimental import pallas as pl
from jax.experimental.pallas import tpu as pltpu
from jax.sharding import PartitionSpec as P

F32, BF16 = jnp.float32, jnp.bfloat16
VMEM = pl.BlockSpec(memory_space=pltpu.VMEM)
HBM = pl.BlockSpec(memory_space=pltpu.HBM)
LIMIT = 24 * 1024 * 1024
HEADS, HD, N = 4, 32, 512
DEVICES = np.arange(512).reshape(8, 16, 2, 2)
FAR = [0] + [6] * 15
OVER_BLOCK = [
    group
    for z in range(16)
    for group in DEVICES[np.arange(8) ^ FAR[z], z].transpose(2, 0, 1).reshape(2, 16).tolist()
]
FIRST_BIAS, FIRST_OUT, STEP = 9, 8, 1
BACK = pow(STEP, -1, 16)


def along_z(first, with_y):
    order = DEVICES[:, (first + STEP * np.arange(16)) % 16]
    return (order.transpose(0, 3, 1, 2).reshape(16, 32) if with_y else order.transpose(0, 2, 3, 1).reshape(32, 16)).tolist()


OVER_CORE = [[0, 1], [2, 3]]
Q, I = 32, 16
MSG = 80
NEAR = 144


def nt(a, b):
    return lax.dot_general(a, b, (((1,), (1,)), ((), ())), preferred_element_type=F32)


def nn(a, b):
    return jnp.dot(a, b, preferred_element_type=F32)


def iota(shape, dim):
    return lax.broadcasted_iota(jnp.int32, shape, dim)


def place():
    row, head = lax.axis_index("row"), lax.axis_index("head")
    return row // 16, head // 2, head % 2, head


def far():
    return jnp.where(lax.axis_index("row") % 16 == 0, FAR[0], FAR[1])


def pack_kernel(
    pair, wq, wk, wv, wg, wb, chain, lists_in, shift_in,
    out, near_out, same_out, sel_out,
    x, w, wb_v, chain_v, lists, shift, halves, message, near, same_v, sel_v, sem,
):
    b, _, core, head = place()
    copies = [
        pltpu.make_async_copy(lists_in, lists, sem.at[0]),
        pltpu.make_async_copy(chain, chain_v, sem.at[1]),
        pltpu.make_async_copy(shift_in, shift, sem.at[2]),
        pltpu.make_async_copy(wb, wb_v, sem.at[3]),
        pltpu.make_async_copy(pair, x, sem.at[4]),
        pltpu.make_async_copy(wq, w.at[0:32], sem.at[5]),
        pltpu.make_async_copy(wk, w.at[32:64], sem.at[6]),
        pltpu.make_async_copy(wv, w.at[64:96], sem.at[7]),
        pltpu.make_async_copy(wg, w.at[96:128], sem.at[8]),
    ]
    for copy in copies:
        copy.start()
    copies[0].wait()
    copies[1].wait()
    b0, b1 = lists[0, b], lists[1, b]
    c0 = jnp.broadcast_to(chain_v[:, pl.ds(pl.multiple_of(b0 // 2 * 128, 128), 128)].astype(F32), (Q, 128))
    c1 = jnp.broadcast_to(chain_v[:, pl.ds(pl.multiple_of(b1 // 2 * 128, 128), 128)].astype(F32), (Q, 128))
    c0 = jnp.where(b0 % 2 == 0, c0, pltpu.roll(c0, 64, 1))
    c1 = jnp.where(b1 % 2 == 1, c1, pltpu.roll(c1, 64, 1))
    key_chain = jnp.where(iota((Q, 128), 1) < 64, c0, c1)
    own = jnp.where(b0 == b, 0, 64)
    p = iota((Q, 128), 0)
    sel = iota((Q, 128), 1) == own + (FIRST_OUT + STEP * (p // 2)) % 16 * 4 + p % 2 * 2 + core
    query_chain = jnp.sum(jnp.where(sel, key_chain, 0.0), axis=-1, keepdims=True)
    same_v[...] = (query_chain == key_chain).astype(F32)
    sel_v[...] = sel.astype(BF16)
    sent = [
        pltpu.make_async_copy(same_v, same_out, sem.at[9]),
        pltpu.make_async_copy(sel_v, sel_out, sem.at[10]),
    ]
    for copy in sent:
        copy.start()
    for copy in copies[2:]:
        copy.wait()
    s = jnp.broadcast_to(shift[...], (16, 128))
    hi = s.astype(BF16).astype(F32)
    mid = (s - hi).astype(BF16).astype(F32)
    low = s - hi - mid
    wide = jnp.broadcast_to(wb_v[...].astype(F32), (16, 128))
    row = iota((16, 128), 0)
    part = row // 4
    small = jnp.where(part == 0, wide, jnp.where(part == 1, hi, jnp.where(part == 2, mid, low)))
    small = jnp.where(row % 4 == head, small, 0.0).astype(BF16)
    w_part = w[pl.ds(pl.multiple_of(b * 16, 16), 16), :]
    flat = x[...].reshape(128, N)
    halves[0] = flat
    for c in range(4):
        halves[1, :, c * 128 : (c + 1) * 128] = pltpu.roll(flat[:, c * 128 : (c + 1) * 128].astype(F32), 64, 1).astype(BF16)
    lane = iota((128, 128), 1)

    def listed(d):
        b0, b1 = lists[0, d], lists[1, d]
        first = halves[b0 % 2, :, pl.ds(pl.multiple_of(b0 // 2 * 128, 128), 128)]
        second = halves[1 - b1 % 2, :, pl.ds(pl.multiple_of(b1 // 2 * 128, 128), 128)]
        return jnp.where(lane < 64, first, second)

    away = far()
    for n in range(8):
        keys = listed(n ^ away)
        start = 2 * n * MSG
        for y in range(2):
            at = start + y * MSG
            message[at : at + 64] = keys[y * 64 : (y + 1) * 64]
            message[at + 64 : at + 80] = w_part
        span = pl.ds(start, 2 * MSG)
        sent.append(pltpu.make_async_copy(message.at[span], out.at[span], sem.at[11 + n]))
        sent[-1].start()
    near[0:128] = listed(b)
    near[128:144] = small
    sent.append(pltpu.make_async_copy(near, near_out, sem.at[19]))
    sent[-1].start()
    for copy in sent:
        copy.wait()


def heads_small(near):
    return sum(near[k, 128:144, :].astype(F32) for k in range(HEADS))


def bias_kernel(near, out):
    core = place()[2]
    small = heads_small(near).astype(BF16)
    found = []
    for y in range(2):
        rows = pl.ds(pl.multiple_of((2 * y + core) * 32, 32), 32)
        found.append(nn(small, jnp.concatenate([near[k, rows, :] for k in range(HEADS)], axis=0))[0:4])
    tile = jnp.concatenate(found * 2, axis=0).astype(BF16)
    for r in range(8):
        out[r * 16 : (r + 1) * 16, :] = tile


def score_kernel(g, near, same, sel, s_out, v_out, gate_out, zq_scr, k_scr):
    small = heads_small(near)
    scale = 1.0 / math.sqrt(HD)
    selector = sel[...]
    away = far()
    w = [
        jnp.concatenate([g[k % 2, 2 * (s ^ away) + k // 2, 64:80, :] for k in range(HEADS) for s in (2 * t, 2 * t + 1)], axis=0)
        for t in range(4)
    ]
    w_kv = jnp.concatenate([w[1], w[2]], axis=0)
    w_qg = jnp.concatenate([w[0], w[3]], axis=0)
    for i in range(I):
        s, t = i // 2, i % 2
        zt = jnp.concatenate([g[k % 2, 2 * s + k // 2, t * 32 : (t + 1) * 32, :] for k in range(HEADS)], axis=0)
        kv = nn(w_kv, zt).astype(BF16)
        k_scr[i] = kv[0:128]
        v_out[i] = kv[128:256]
        zq_scr[i * Q : (i + 1) * Q] = nt(selector, zt).astype(BF16)
    qg = nt(zq_scr[...], w_qg).astype(BF16)
    gate_out[...] = qg[:, 128:256]
    head_of_lane = iota((Q, 128), 1) // HD
    moved = jnp.concatenate(
        [same[...] * (small[4 + k : 5 + k] + small[8 + k : 9 + k] + small[12 + k : 13 + k]) for k in range(HEADS)], axis=0
    )
    for i in range(I):
        q = qg[i * Q : (i + 1) * Q, 0:128]
        zero = jnp.zeros_like(q)
        q_all = jnp.concatenate([jnp.where(head_of_lane == k, q, zero) for k in range(HEADS)], axis=0)
        s_out[i] = nn(q_all, k_scr[i]) * scale + moved


def mix_kernel(bias, s_in, v, gate, w_out, out, acc):
    row = iota((128, 128), 0)
    n = (row % Q // 2 + BACK * (FIRST_OUT - FIRST_BIAS + 16)) % 16
    perm = (iota((128, 128), 1) == (2 * n + row % 2) * 4 + row // Q).astype(BF16)
    head_of_lane = iota((Q, 128), 1) // HD
    plane = nn(perm, bias[...])
    away = far()
    for i in range(I):
        s = s_in[i] + plane
        e = jnp.exp(s - jnp.max(s, axis=-1, keepdims=True))
        p = (e * (1.0 / jnp.sum(e, axis=-1, keepdims=True))).astype(BF16)
        every = nt(p, v[i])
        o = every[0:Q]
        for k in range(1, HEADS):
            o = jnp.where(head_of_lane == k, every[k * Q : (k + 1) * Q], o)
        acc[pl.ds((i // 2 ^ away) * 2 + i % 2, Q, stride=I), :] = jax.nn.sigmoid(gate[i * Q : (i + 1) * Q, :].astype(F32)) * o
    out[...] = nn(acc[...].astype(BF16), w_out[...]).astype(BF16)


def order_kernel(moved, out, before, after):
    before[...] = moved[...].astype(F32)
    for p in range(32):
        z = (FIRST_OUT + STEP * (p // 2)) % 16
        for t in range(2):
            after[pl.ds(4 * z + 2 * (p % 2) + t, 8, stride=64), :] = before[pl.ds(p * 16 + t, 8, stride=2), :]
    out[...] = after[...].astype(BF16)


def call(kernel, ins, outs, scratch=(), flops=0, nbytes=0):
    return pl.pallas_call(
        kernel,
        in_specs=ins,
        out_specs=[VMEM] * len(outs) if isinstance(outs, list) else VMEM,
        out_shape=outs,
        scratch_shapes=list(scratch),
        compiler_params=pltpu.CompilerParams(vmem_limit_bytes=LIMIT),
        cost_estimate=pl.CostEstimate(flops=flops, bytes_accessed=nbytes, transcendentals=0),
    )


def local(pair, w_query, w_key, w_value, w_gate, w_bias, w_out, shift, block_lists, chain_ids):
    shape = jax.ShapeDtypeStruct
    packed, near, same, sel = pl.pallas_call(
        pack_kernel,
        in_specs=[HBM] * 9,
        out_specs=[HBM] * 4,
        out_shape=[shape((16 * MSG, 128), BF16), shape((NEAR, 128), BF16), shape((Q, 128), F32), shape((Q, 128), BF16)],
        scratch_shapes=[
            pltpu.VMEM((4, 32, N), BF16),
            pltpu.VMEM((128, 128), BF16),
            pltpu.VMEM((1, 128), BF16),
            pltpu.VMEM((1, N), jnp.int32),
            pltpu.SMEM((2, 8), jnp.int32),
            pltpu.VMEM((1, 1), F32),
            pltpu.VMEM((2, 128, N), BF16),
            pltpu.VMEM((16 * MSG, 128), BF16),
            pltpu.VMEM((NEAR, 128), BF16),
            pltpu.VMEM((Q, 128), F32),
            pltpu.VMEM((Q, 128), BF16),
            pltpu.SemaphoreType.DMA((20,)),
        ],
        cost_estimate=pl.CostEstimate(flops=0, bytes_accessed=1000000, transcendentals=0),
    )(
        pair.transpose(0, 2, 1), w_query.T, w_key.T, w_value.T, w_gate.T, w_bias.T,
        chain_ids.reshape(1, N), block_lists.T, shift.reshape(1, 1),
    )
    got = lax.all_to_all(
        packed.reshape(16, MSG, 128), ("row", "head"), 0, 0, tiled=True, axis_index_groups=OVER_BLOCK
    )
    g = lax.all_gather(got, "head", axis=0, axis_index_groups=OVER_CORE)
    near = lax.all_gather(near, "head", axis=0)
    mine = call(bias_kernel, [VMEM], shape((128, 128), BF16), nbytes=400000)(near)
    bias = lax.all_to_all(
        mine.reshape(16, 8, 128), ("row", "head"), 0, 0, tiled=True, axis_index_groups=along_z(FIRST_BIAS, False)
    ).reshape(128, 128)
    scores, v, gate = call(
        score_kernel,
        [VMEM] * 4,
        [shape((I, 128, 128), F32), shape((I, 128, 128), BF16), shape((I * Q, 128), BF16)],
        [pltpu.VMEM((I * Q, 128), BF16), pltpu.VMEM((I, 128, 128), BF16)],
        flops=1000000000,
        nbytes=4000000,
    )(g, near, same, sel)
    mixed = call(
        mix_kernel,
        [VMEM] * 5,
        shape((I * Q, 128), BF16),
        [pltpu.VMEM((I * Q, 128), F32)],
        flops=100000000,
        nbytes=3000000,
    )(bias, scores, v, gate, w_out)
    moved = lax.all_to_all(
        mixed.reshape(32, I, 128), ("row", "head"), 0, 0, tiled=True, axis_index_groups=along_z(FIRST_OUT, True)
    ).reshape(512, 128)
    ordered = call(
        order_kernel, [VMEM], shape((512, 128), BF16), [pltpu.VMEM((512, 128), F32)] * 2, nbytes=300000
    )(moved)
    return ordered.reshape(512, 1, 128)


def solution(mesh):
    in_specs = (
        P("row", None, "head"),
        P(None, "head"),
        P(None, "head"),
        P(None, "head"),
        P(None, "head"),
        P(None, "head"),
        P(),
        P("head"),
        P(),
        P(),
    )
    out_specs = P(None, ("row", "head"), None)
    return jax.shard_map(local, mesh=mesh, in_specs=in_specs, out_specs=out_specs, check_vma=False)
```

```python
import math

import jax
import jax.numpy as jnp
import numpy as np
from jax import lax
from jax.experimental import pallas as pl
from jax.experimental.pallas import tpu as pltpu
from jax.sharding import PartitionSpec as P

F32, BF16 = jnp.float32, jnp.bfloat16
VMEM = pl.BlockSpec(memory_space=pltpu.VMEM)
HBM = pl.BlockSpec(memory_space=pltpu.HBM)
LIMIT = 24 * 1024 * 1024
HEADS, HD, N = 4, 32, 512
DEVICES = np.arange(512).reshape(8, 16, 2, 2)
FAR = [0] + [6] * 15
OVER_BLOCK = [
    group
    for z in range(16)
    for group in DEVICES[np.arange(8) ^ FAR[z], z].transpose(2, 0, 1).reshape(2, 16).tolist()
]
FIRST_BIAS, FIRST_OUT = 11, 8


def along_z(first, with_y):
    order = DEVICES[:, (first + np.arange(16)) % 16]
    return (order.transpose(0, 3, 1, 2).reshape(16, 32) if with_y else order.transpose(0, 2, 3, 1).reshape(32, 16)).tolist()


OVER_CORE = [[0, 1], [2, 3]]
Q, I = 32, 16
MSG = 80
NEAR = 144


def nt(a, b):
    return lax.dot_general(a, b, (((1,), (1,)), ((), ())), preferred_element_type=F32)


def nn(a, b):
    return jnp.dot(a, b, preferred_element_type=F32)


def iota(shape, dim):
    return lax.broadcasted_iota(jnp.int32, shape, dim)


def place():
    row, head = lax.axis_index("row"), lax.axis_index("head")
    return row // 16, head // 2, head % 2, head


def far():
    return jnp.where(lax.axis_index("row") % 16 == 0, FAR[0], FAR[1])


def pack_kernel(
    pair, wq, wk, wv, wg, wb, chain, lists_in, shift_in,
    out, near_out, same_out, sel_out,
    x, w, wb_v, chain_v, lists, shift, halves, message, near, same_v, sel_v, sem,
):
    b, _, core, head = place()
    copies = [
        pltpu.make_async_copy(lists_in, lists, sem.at[0]),
        pltpu.make_async_copy(chain, chain_v, sem.at[1]),
        pltpu.make_async_copy(shift_in, shift, sem.at[2]),
        pltpu.make_async_copy(wb, wb_v, sem.at[3]),
        pltpu.make_async_copy(pair, x, sem.at[4]),
        pltpu.make_async_copy(wq, w.at[0:32], sem.at[5]),
        pltpu.make_async_copy(wk, w.at[32:64], sem.at[6]),
        pltpu.make_async_copy(wv, w.at[64:96], sem.at[7]),
        pltpu.make_async_copy(wg, w.at[96:128], sem.at[8]),
    ]
    for copy in copies:
        copy.start()
    copies[0].wait()
    copies[1].wait()
    b0, b1 = lists[0, b], lists[1, b]
    c0 = jnp.broadcast_to(chain_v[:, pl.ds(pl.multiple_of(b0 // 2 * 128, 128), 128)].astype(F32), (Q, 128))
    c1 = jnp.broadcast_to(chain_v[:, pl.ds(pl.multiple_of(b1 // 2 * 128, 128), 128)].astype(F32), (Q, 128))
    c0 = jnp.where(b0 % 2 == 0, c0, pltpu.roll(c0, 64, 1))
    c1 = jnp.where(b1 % 2 == 1, c1, pltpu.roll(c1, 64, 1))
    key_chain = jnp.where(iota((Q, 128), 1) < 64, c0, c1)
    own = jnp.where(b0 == b, 0, 64)
    p = iota((Q, 128), 0)
    sel = iota((Q, 128), 1) == own + (FIRST_OUT + p // 2) % 16 * 4 + p % 2 * 2 + core
    query_chain = jnp.sum(jnp.where(sel, key_chain, 0.0), axis=-1, keepdims=True)
    same_v[...] = (query_chain == key_chain).astype(F32)
    sel_v[...] = sel.astype(BF16)
    sent = [
        pltpu.make_async_copy(same_v, same_out, sem.at[9]),
        pltpu.make_async_copy(sel_v, sel_out, sem.at[10]),
    ]
    for copy in sent:
        copy.start()
    for copy in copies[2:]:
        copy.wait()
    s = jnp.broadcast_to(shift[...], (16, 128))
    hi = s.astype(BF16).astype(F32)
    mid = (s - hi).astype(BF16).astype(F32)
    low = s - hi - mid
    wide = jnp.broadcast_to(wb_v[...].astype(F32), (16, 128))
    row = iota((16, 128), 0)
    part = row // 4
    small = jnp.where(part == 0, wide, jnp.where(part == 1, hi, jnp.where(part == 2, mid, low)))
    small = jnp.where(row % 4 == head, small, 0.0).astype(BF16)
    w_part = w[pl.ds(pl.multiple_of(b * 16, 16), 16), :]
    flat = x[...].reshape(128, N)
    halves[0] = flat
    for c in range(4):
        halves[1, :, c * 128 : (c + 1) * 128] = pltpu.roll(flat[:, c * 128 : (c + 1) * 128].astype(F32), 64, 1).astype(BF16)
    lane = iota((128, 128), 1)

    def listed(d):
        b0, b1 = lists[0, d], lists[1, d]
        first = halves[b0 % 2, :, pl.ds(pl.multiple_of(b0 // 2 * 128, 128), 128)]
        second = halves[1 - b1 % 2, :, pl.ds(pl.multiple_of(b1 // 2 * 128, 128), 128)]
        return jnp.where(lane < 64, first, second)

    near[0:128] = listed(b)
    near[128:144] = small
    sent.append(pltpu.make_async_copy(near, near_out, sem.at[19]))
    sent[-1].start()
    away = far()
    for n in range(8):
        keys = listed(n ^ away)
        start = 2 * n * MSG
        for y in range(2):
            at = start + y * MSG
            message[at : at + 64] = keys[y * 64 : (y + 1) * 64]
            message[at + 64 : at + 80] = w_part
        span = pl.ds(start, 2 * MSG)
        sent.append(pltpu.make_async_copy(message.at[span], out.at[span], sem.at[11 + n]))
        sent[-1].start()
    for copy in sent:
        copy.wait()


def heads_small(near):
    return sum(near[k, 128:144, :].astype(F32) for k in range(HEADS))


def bias_kernel(near, out):
    core = place()[2]
    small = heads_small(near).astype(BF16)
    found = []
    for y in range(2):
        rows = pl.ds(pl.multiple_of((2 * y + core) * 32, 32), 32)
        found.append(nn(small, jnp.concatenate([near[k, rows, :] for k in range(HEADS)], axis=0))[0:4])
    tile = jnp.concatenate(found * 2, axis=0).astype(BF16)
    for r in range(8):
        out[r * 16 : (r + 1) * 16, :] = tile


def score_kernel(g, near, same, sel, s_out, v_out, gate_out, zq_scr, k_scr):
    small = heads_small(near)
    scale = 1.0 / math.sqrt(HD)
    selector = sel[...]
    away = far()
    w = [
        jnp.concatenate([g[k % 2, 2 * (s ^ away) + k // 2, 64:80, :] for k in range(HEADS) for s in (2 * t, 2 * t + 1)], axis=0)
        for t in range(4)
    ]
    w_kv = jnp.concatenate([w[1], w[2]], axis=0)
    w_qg = jnp.concatenate([w[0], w[3]], axis=0)
    for i in range(I):
        s, t = i // 2, i % 2
        zt = jnp.concatenate([g[k % 2, 2 * s + k // 2, t * 32 : (t + 1) * 32, :] for k in range(HEADS)], axis=0)
        kv = nn(w_kv, zt).astype(BF16)
        k_scr[i] = kv[0:128]
        v_out[i] = kv[128:256]
        zq_scr[i * Q : (i + 1) * Q] = nt(selector, zt).astype(BF16)
    qg = nt(zq_scr[...], w_qg).astype(BF16)
    gate_out[...] = qg[:, 128:256]
    head_of_lane = iota((Q, 128), 1) // HD
    moved = jnp.concatenate(
        [same[...] * (small[4 + k : 5 + k] + small[8 + k : 9 + k] + small[12 + k : 13 + k]) for k in range(HEADS)], axis=0
    )
    for i in range(I):
        q = qg[i * Q : (i + 1) * Q, 0:128]
        zero = jnp.zeros_like(q)
        q_all = jnp.concatenate([jnp.where(head_of_lane == k, q, zero) for k in range(HEADS)], axis=0)
        s_out[i] = nn(q_all, k_scr[i]) * scale + moved


def mix_kernel(bias, s_in, v, gate, w_out, out, acc):
    row = iota((128, 128), 0)
    n = (row % Q // 2 + FIRST_OUT - FIRST_BIAS + 16) % 16
    perm = (iota((128, 128), 1) == (2 * n + row % 2) * 4 + row // Q).astype(BF16)
    head_of_lane = iota((Q, 128), 1) // HD
    plane = nn(perm, bias[...])
    away = far()
    for i in range(I):
        s = s_in[i] + plane
        e = jnp.exp(s - jnp.max(s, axis=-1, keepdims=True))
        p = (e * (1.0 / jnp.sum(e, axis=-1, keepdims=True))).astype(BF16)
        every = nt(p, v[i])
        o = every[0:Q]
        for k in range(1, HEADS):
            o = jnp.where(head_of_lane == k, every[k * Q : (k + 1) * Q], o)
        acc[pl.ds((i // 2 ^ away) * 2 + i % 2, Q, stride=I), :] = jax.nn.sigmoid(gate[i * Q : (i + 1) * Q, :].astype(F32)) * o
    out[...] = nn(acc[...].astype(BF16), w_out[...]).astype(BF16)


def order_kernel(moved, out, before, after, stage, sem):
    before[...] = moved[...].astype(F32)
    turn, left = 2 * FIRST_OUT, 32 - 2 * FIRST_OUT
    copies = []
    for s in range(8):
        for t in range(2):
            after[pl.ds(s * 64 + 2 * turn + t, left, stride=2), :] = before[pl.ds(2 * s + t, left, stride=16), :]
            after[pl.ds(s * 64 + t, turn, stride=2), :] = before[pl.ds(left * 16 + 2 * s + t, turn, stride=16), :]
        span = pl.ds(s * 64, 64)
        stage[span, :] = after[span, :].astype(BF16)
        copies.append(pltpu.make_async_copy(stage.at[span], out.at[span], sem.at[s]))
        copies[-1].start()
    for copy in copies:
        copy.wait()


def call(kernel, ins, outs, scratch=(), flops=0, nbytes=0):
    return pl.pallas_call(
        kernel,
        in_specs=ins,
        out_specs=[VMEM] * len(outs) if isinstance(outs, list) else VMEM,
        out_shape=outs,
        scratch_shapes=list(scratch),
        compiler_params=pltpu.CompilerParams(vmem_limit_bytes=LIMIT),
        cost_estimate=pl.CostEstimate(flops=flops, bytes_accessed=nbytes, transcendentals=0),
    )


def local(pair, w_query, w_key, w_value, w_gate, w_bias, w_out, shift, block_lists, chain_ids):
    shape = jax.ShapeDtypeStruct
    packed, near, same, sel = pl.pallas_call(
        pack_kernel,
        in_specs=[HBM] * 9,
        out_specs=[HBM] * 4,
        out_shape=[shape((16 * MSG, 128), BF16), shape((NEAR, 128), BF16), shape((Q, 128), F32), shape((Q, 128), BF16)],
        scratch_shapes=[
            pltpu.VMEM((4, 32, N), BF16),
            pltpu.VMEM((128, 128), BF16),
            pltpu.VMEM((1, 128), BF16),
            pltpu.VMEM((1, N), jnp.int32),
            pltpu.SMEM((2, 8), jnp.int32),
            pltpu.VMEM((1, 1), F32),
            pltpu.VMEM((2, 128, N), BF16),
            pltpu.VMEM((16 * MSG, 128), BF16),
            pltpu.VMEM((NEAR, 128), BF16),
            pltpu.VMEM((Q, 128), F32),
            pltpu.VMEM((Q, 128), BF16),
            pltpu.SemaphoreType.DMA((20,)),
        ],
        cost_estimate=pl.CostEstimate(flops=0, bytes_accessed=1000000, transcendentals=0),
    )(
        pair.transpose(0, 2, 1), w_query.T, w_key.T, w_value.T, w_gate.T, w_bias.T,
        chain_ids.reshape(1, N), block_lists.T, shift.reshape(1, 1),
    )
    got = lax.all_to_all(
        packed.reshape(16, MSG, 128), ("row", "head"), 0, 0, tiled=True, axis_index_groups=OVER_BLOCK
    )
    g = lax.all_gather(got, "head", axis=0, axis_index_groups=OVER_CORE)
    near = lax.all_gather(near, "head", axis=0)
    mine = call(bias_kernel, [VMEM], shape((128, 128), BF16), nbytes=400000)(near)
    bias = lax.all_to_all(
        mine.reshape(16, 8, 128), ("row", "head"), 0, 0, tiled=True, axis_index_groups=along_z(FIRST_BIAS, False)
    ).reshape(128, 128)
    scores, v, gate = call(
        score_kernel,
        [VMEM] * 4,
        [shape((I, 128, 128), F32), shape((I, 128, 128), BF16), shape((I * Q, 128), BF16)],
        [pltpu.VMEM((I * Q, 128), BF16), pltpu.VMEM((I, 128, 128), BF16)],
        flops=1000000000,
        nbytes=4000000,
    )(g, near, same, sel)
    mixed = call(
        mix_kernel,
        [VMEM] * 5,
        shape((I * Q, 128), BF16),
        [pltpu.VMEM((I * Q, 128), F32)],
        flops=100000000,
        nbytes=3000000,
    )(bias, scores, v, gate, w_out)
    moved = lax.all_to_all(
        mixed.reshape(32, I, 128), ("row", "head"), 0, 0, tiled=True, axis_index_groups=along_z(FIRST_OUT, True)
    ).reshape(512, 128)
    ordered = pl.pallas_call(
        order_kernel,
        in_specs=[VMEM],
        out_specs=HBM,
        out_shape=shape((512, 128), BF16),
        scratch_shapes=[
            pltpu.VMEM((512, 128), F32),
            pltpu.VMEM((512, 128), F32),
            pltpu.VMEM((512, 128), BF16),
            pltpu.SemaphoreType.DMA((8,)),
        ],
        compiler_params=pltpu.CompilerParams(vmem_limit_bytes=LIMIT),
        cost_estimate=pl.CostEstimate(flops=0, bytes_accessed=300000, transcendentals=0),
    )(moved)
    return ordered.reshape(512, 1, 128)


def solution(mesh):
    in_specs = (
        P("row", None, "head"),
        P(None, "head"),
        P(None, "head"),
        P(None, "head"),
        P(None, "head"),
        P(None, "head"),
        P(),
        P("head"),
        P(),
        P(),
    )
    out_specs = P(None, ("row", "head"), None)
    return jax.shard_map(local, mesh=mesh, in_specs=in_specs, out_specs=out_specs, check_vma=False)
```

```python
import math

import jax
import jax.numpy as jnp
import numpy as np
from jax import lax
from jax.experimental import pallas as pl
from jax.experimental.pallas import tpu as pltpu
from jax.sharding import PartitionSpec as P

F32, BF16 = jnp.float32, jnp.bfloat16
VMEM = pl.BlockSpec(memory_space=pltpu.VMEM)
HBM = pl.BlockSpec(memory_space=pltpu.HBM)
LIMIT = 24 * 1024 * 1024
HEADS, HD, N = 4, 32, 512
DEVICES = np.arange(512).reshape(8, 16, 2, 2)
FAR = [0] + [6] * 15
OVER_BLOCK = [
    group
    for z in range(16)
    for group in DEVICES[np.arange(8) ^ FAR[z], z].transpose(2, 0, 1).reshape(2, 16).tolist()
]
FIRST_BIAS, FIRST_OUT = 11, 8


def along_z(first, with_y):
    order = DEVICES[:, (first + np.arange(16)) % 16]
    return (order.transpose(0, 3, 1, 2).reshape(16, 32) if with_y else order.transpose(0, 2, 3, 1).reshape(32, 16)).tolist()


OVER_CORE = [[0, 1], [2, 3]]
Q, I = 32, 16
MSG = 80
NEAR = 144


def nt(a, b):
    return lax.dot_general(a, b, (((1,), (1,)), ((), ())), preferred_element_type=F32)


def nn(a, b):
    return jnp.dot(a, b, preferred_element_type=F32)


def iota(shape, dim):
    return lax.broadcasted_iota(jnp.int32, shape, dim)


def place():
    row, head = lax.axis_index("row"), lax.axis_index("head")
    return row // 16, head // 2, head % 2, head


def far():
    return jnp.where(lax.axis_index("row") % 16 == 0, FAR[0], FAR[1])


def pack_kernel(
    pair, wq, wk, wv, wg, wb, chain, lists_in, shift_in,
    out, near_out, same_out, sel_out,
    x, w, wb_v, chain_v, lists, shift, halves, message, near, same_v, sel_v, sem,
):
    b, _, core, head = place()
    copies = [
        pltpu.make_async_copy(lists_in, lists, sem.at[0]),
        pltpu.make_async_copy(chain, chain_v, sem.at[1]),
        pltpu.make_async_copy(shift_in, shift, sem.at[2]),
        pltpu.make_async_copy(wb, wb_v, sem.at[3]),
        pltpu.make_async_copy(pair, x, sem.at[4]),
        pltpu.make_async_copy(wq, w.at[0:32], sem.at[5]),
        pltpu.make_async_copy(wk, w.at[32:64], sem.at[6]),
        pltpu.make_async_copy(wv, w.at[64:96], sem.at[7]),
        pltpu.make_async_copy(wg, w.at[96:128], sem.at[8]),
    ]
    for copy in copies:
        copy.start()
    copies[0].wait()
    copies[1].wait()
    b0, b1 = lists[0, b], lists[1, b]
    c0 = jnp.broadcast_to(chain_v[:, pl.ds(pl.multiple_of(b0 // 2 * 128, 128), 128)].astype(F32), (Q, 128))
    c1 = jnp.broadcast_to(chain_v[:, pl.ds(pl.multiple_of(b1 // 2 * 128, 128), 128)].astype(F32), (Q, 128))
    c0 = jnp.where(b0 % 2 == 0, c0, pltpu.roll(c0, 64, 1))
    c1 = jnp.where(b1 % 2 == 1, c1, pltpu.roll(c1, 64, 1))
    key_chain = jnp.where(iota((Q, 128), 1) < 64, c0, c1)
    own = jnp.where(b0 == b, 0, 64)
    p = iota((Q, 128), 0)
    sel = iota((Q, 128), 1) == own + (FIRST_OUT + p // 2) % 16 * 4 + p % 2 * 2 + core
    query_chain = jnp.sum(jnp.where(sel, key_chain, 0.0), axis=-1, keepdims=True)
    same_v[...] = (query_chain == key_chain).astype(F32)
    sel_v[...] = sel.astype(BF16)
    sent = [
        pltpu.make_async_copy(same_v, same_out, sem.at[9]),
        pltpu.make_async_copy(sel_v, sel_out, sem.at[10]),
    ]
    for copy in sent:
        copy.start()
    for copy in copies[2:]:
        copy.wait()
    s = jnp.broadcast_to(shift[...], (16, 128))
    hi = s.astype(BF16).astype(F32)
    mid = (s - hi).astype(BF16).astype(F32)
    low = s - hi - mid
    wide = jnp.broadcast_to(wb_v[...].astype(F32), (16, 128))
    row = iota((16, 128), 0)
    part = row // 4
    small = jnp.where(part == 0, wide, jnp.where(part == 1, hi, jnp.where(part == 2, mid, low)))
    small = jnp.where(row % 4 == head, small, 0.0).astype(BF16)
    w_part = w[pl.ds(pl.multiple_of(b * 16, 16), 16), :]
    flat = x[...].reshape(128, N)
    halves[0] = flat
    for c in range(4):
        halves[1, :, c * 128 : (c + 1) * 128] = pltpu.roll(flat[:, c * 128 : (c + 1) * 128].astype(F32), 64, 1).astype(BF16)
    lane = iota((128, 128), 1)

    def listed(d):
        b0, b1 = lists[0, d], lists[1, d]
        first = halves[b0 % 2, :, pl.ds(pl.multiple_of(b0 // 2 * 128, 128), 128)]
        second = halves[1 - b1 % 2, :, pl.ds(pl.multiple_of(b1 // 2 * 128, 128), 128)]
        return jnp.where(lane < 64, first, second)

    near[0:128] = listed(b)
    near[128:144] = small
    sent.append(pltpu.make_async_copy(near, near_out, sem.at[19]))
    sent[-1].start()
    away = far()
    for n in range(8):
        keys = listed(n ^ away)
        start = 2 * n * MSG
        for y in range(2):
            at = start + y * MSG
            message[at : at + 64] = keys[y * 64 : (y + 1) * 64]
            message[at + 64 : at + 80] = w_part
        span = pl.ds(start, 2 * MSG)
        sent.append(pltpu.make_async_copy(message.at[span], out.at[span], sem.at[11 + n]))
        sent[-1].start()
    for copy in sent:
        copy.wait()


def heads_small(near):
    return sum(near[k, 128:144, :].astype(F32) for k in range(HEADS))


def bias_kernel(near, out):
    core = place()[2]
    small = heads_small(near).astype(BF16)
    found = []
    for y in range(2):
        rows = pl.ds(pl.multiple_of((2 * y + core) * 32, 32), 32)
        found.append(nn(small, jnp.concatenate([near[k, rows, :] for k in range(HEADS)], axis=0))[0:4])
    tile = jnp.concatenate(found * 2, axis=0).astype(BF16)
    for r in range(8):
        out[r * 16 : (r + 1) * 16, :] = tile


def score_kernel(g, near, same, sel, s_out, v_out, gate_out, moved_out, zq_scr, k_scr):
    small = heads_small(near)
    scale = 1.0 / math.sqrt(HD)
    selector = sel[...]
    away = far()
    w = [
        jnp.concatenate([g[k % 2, 2 * (s ^ away) + k // 2, 64:80, :] for k in range(HEADS) for s in (2 * t, 2 * t + 1)], axis=0)
        for t in range(4)
    ]
    w_kv = jnp.concatenate([w[1], w[2]], axis=0)
    w_qg = jnp.concatenate([w[0], w[3]], axis=0)
    for i in range(I):
        s, t = i // 2, i % 2
        zt = jnp.concatenate([g[k % 2, 2 * s + k // 2, t * 32 : (t + 1) * 32, :] for k in range(HEADS)], axis=0)
        kv = nn(w_kv, zt).astype(BF16)
        k_scr[i] = kv[0:128]
        v_out[i] = kv[128:256]
        zq_scr[i * Q : (i + 1) * Q] = nt(selector, zt).astype(BF16)
    qg = nt(zq_scr[...], w_qg).astype(BF16)
    gate_out[...] = qg[:, 128:256]
    head_of_lane = iota((Q, 128), 1) // HD
    moved_out[...] = jnp.concatenate(
        [same[...] * (small[4 + k : 5 + k] + small[8 + k : 9 + k] + small[12 + k : 13 + k]) for k in range(HEADS)], axis=0
    )
    for i in range(I):
        q = qg[i * Q : (i + 1) * Q, 0:128]
        zero = jnp.zeros_like(q)
        q_all = jnp.concatenate([jnp.where(head_of_lane == k, q, zero) for k in range(HEADS)], axis=0)
        s_out[i] = nn(q_all, k_scr[i]) * scale


def mix_kernel(bias, s_in, v, gate, moved, w_out, out, acc):
    row = iota((128, 128), 0)
    n = (row % Q // 2 + FIRST_OUT - FIRST_BIAS + 16) % 16
    perm = (iota((128, 128), 1) == (2 * n + row % 2) * 4 + row // Q).astype(BF16)
    head_of_lane = iota((Q, 128), 1) // HD
    logit_bias = nn(perm, bias[...]) + moved[...]
    away = far()
    for i in range(I):
        s = s_in[i] + logit_bias
        e = jnp.exp(s - jnp.max(s, axis=-1, keepdims=True))
        p = (e * (1.0 / jnp.sum(e, axis=-1, keepdims=True))).astype(BF16)
        every = nt(p, v[i])
        o = every[0:Q]
        for k in range(1, HEADS):
            o = jnp.where(head_of_lane == k, every[k * Q : (k + 1) * Q], o)
        acc[pl.ds((i // 2 ^ away) * 2 + i % 2, Q, stride=I), :] = jax.nn.sigmoid(gate[i * Q : (i + 1) * Q, :].astype(F32)) * o
    out[...] = nn(acc[...].astype(BF16), w_out[...]).astype(BF16)


def order_kernel(moved, out, before, after, stage, sem):
    before[...] = moved[...].astype(F32)
    turn, left = 2 * FIRST_OUT, 32 - 2 * FIRST_OUT
    copies = []
    for s in range(8):
        for t in range(2):
            after[pl.ds(s * 64 + 2 * turn + t, left, stride=2), :] = before[pl.ds(2 * s + t, left, stride=16), :]
            after[pl.ds(s * 64 + t, turn, stride=2), :] = before[pl.ds(left * 16 + 2 * s + t, turn, stride=16), :]
        span = pl.ds(s * 64, 64)
        stage[span, :] = after[span, :].astype(BF16)
        copies.append(pltpu.make_async_copy(stage.at[span], out.at[span], sem.at[s]))
        copies[-1].start()
    for copy in copies:
        copy.wait()


def call(kernel, ins, outs, scratch=(), flops=0, nbytes=0):
    return pl.pallas_call(
        kernel,
        in_specs=ins,
        out_specs=[VMEM] * len(outs) if isinstance(outs, list) else VMEM,
        out_shape=outs,
        scratch_shapes=list(scratch),
        compiler_params=pltpu.CompilerParams(vmem_limit_bytes=LIMIT),
        cost_estimate=pl.CostEstimate(flops=flops, bytes_accessed=nbytes, transcendentals=0),
    )


def local(pair, w_query, w_key, w_value, w_gate, w_bias, w_out, shift, block_lists, chain_ids):
    shape = jax.ShapeDtypeStruct
    packed, near, same, sel = pl.pallas_call(
        pack_kernel,
        in_specs=[HBM] * 9,
        out_specs=[HBM] * 4,
        out_shape=[shape((16 * MSG, 128), BF16), shape((NEAR, 128), BF16), shape((Q, 128), F32), shape((Q, 128), BF16)],
        scratch_shapes=[
            pltpu.VMEM((4, 32, N), BF16),
            pltpu.VMEM((128, 128), BF16),
            pltpu.VMEM((1, 128), BF16),
            pltpu.VMEM((1, N), jnp.int32),
            pltpu.SMEM((2, 8), jnp.int32),
            pltpu.VMEM((1, 1), F32),
            pltpu.VMEM((2, 128, N), BF16),
            pltpu.VMEM((16 * MSG, 128), BF16),
            pltpu.VMEM((NEAR, 128), BF16),
            pltpu.VMEM((Q, 128), F32),
            pltpu.VMEM((Q, 128), BF16),
            pltpu.SemaphoreType.DMA((20,)),
        ],
        cost_estimate=pl.CostEstimate(flops=0, bytes_accessed=1000000, transcendentals=0),
    )(
        pair.transpose(0, 2, 1), w_query.T, w_key.T, w_value.T, w_gate.T, w_bias.T,
        chain_ids.reshape(1, N), block_lists.T, shift.reshape(1, 1),
    )
    got = lax.all_to_all(
        packed.reshape(16, MSG, 128), ("row", "head"), 0, 0, tiled=True, axis_index_groups=OVER_BLOCK
    )
    g = lax.all_gather(got, "head", axis=0, axis_index_groups=OVER_CORE)
    near = lax.all_gather(near, "head", axis=0)
    mine = call(bias_kernel, [VMEM], shape((128, 128), BF16), nbytes=400000)(near)
    bias = lax.all_to_all(
        mine.reshape(16, 8, 128), ("row", "head"), 0, 0, tiled=True, axis_index_groups=along_z(FIRST_BIAS, False)
    ).reshape(128, 128)
    scores, v, gate, moved = call(
        score_kernel,
        [VMEM] * 4,
        [shape((I, 128, 128), F32), shape((I, 128, 128), BF16), shape((I * Q, 128), BF16), shape((128, 128), F32)],
        [pltpu.VMEM((I * Q, 128), BF16), pltpu.VMEM((I, 128, 128), BF16)],
        flops=1000000000,
        nbytes=4000000,
    )(g, near, same, sel)
    mixed = call(
        mix_kernel,
        [VMEM] * 6,
        shape((I * Q, 128), BF16),
        [pltpu.VMEM((I * Q, 128), F32)],
        flops=100000000,
        nbytes=3000000,
    )(bias, scores, v, gate, moved, w_out)
    arrived = lax.all_to_all(
        mixed.reshape(32, I, 128), ("row", "head"), 0, 0, tiled=True, axis_index_groups=along_z(FIRST_OUT, True)
    ).reshape(512, 128)
    ordered = pl.pallas_call(
        order_kernel,
        in_specs=[VMEM],
        out_specs=HBM,
        out_shape=shape((512, 128), BF16),
        scratch_shapes=[
            pltpu.VMEM((512, 128), F32),
            pltpu.VMEM((512, 128), F32),
            pltpu.VMEM((512, 128), BF16),
            pltpu.SemaphoreType.DMA((8,)),
        ],
        compiler_params=pltpu.CompilerParams(vmem_limit_bytes=LIMIT),
        cost_estimate=pl.CostEstimate(flops=0, bytes_accessed=300000, transcendentals=0),
    )(arrived)
    return ordered.reshape(512, 1, 128)


def solution(mesh):
    in_specs = (
        P("row", None, "head"),
        P(None, "head"),
        P(None, "head"),
        P(None, "head"),
        P(None, "head"),
        P(None, "head"),
        P(),
        P("head"),
        P(),
        P(),
    )
    out_specs = P(None, ("row", "head"), None)
    return jax.shard_map(local, mesh=mesh, in_specs=in_specs, out_specs=out_specs, check_vma=False)
```

```python
import math

import jax
import jax.numpy as jnp
import numpy as np
from jax import lax
from jax.experimental import pallas as pl
from jax.experimental.pallas import tpu as pltpu
from jax.sharding import PartitionSpec as P

F32, BF16 = jnp.float32, jnp.bfloat16
VMEM = pl.BlockSpec(memory_space=pltpu.VMEM)
HBM = pl.BlockSpec(memory_space=pltpu.HBM)
LIMIT = 24 * 1024 * 1024
HEADS, HD, N = 4, 32, 512
DEVICES = np.arange(512).reshape(8, 16, 2, 2)
FAR = [0] + [6] * 15
OVER_BLOCK = [
    group
    for z in range(16)
    for group in DEVICES[np.arange(8) ^ FAR[z], z].transpose(2, 0, 1).reshape(2, 16).tolist()
]
FIRST_BIAS, FIRST_OUT = 11, 8


def along_z(first, with_y):
    order = DEVICES[:, (first + np.arange(16)) % 16]
    return (order.transpose(0, 3, 1, 2).reshape(16, 32) if with_y else order.transpose(0, 2, 3, 1).reshape(32, 16)).tolist()


OVER_CORE = [[0, 1], [2, 3]]
Q, I = 32, 16
MSG = 80
NEAR = 144


def nt(a, b):
    return lax.dot_general(a, b, (((1,), (1,)), ((), ())), preferred_element_type=F32)


def nn(a, b):
    return jnp.dot(a, b, preferred_element_type=F32)


def iota(shape, dim):
    return lax.broadcasted_iota(jnp.int32, shape, dim)


def place():
    row, head = lax.axis_index("row"), lax.axis_index("head")
    return row // 16, head // 2, head % 2, head


def far():
    return jnp.where(lax.axis_index("row") % 16 == 0, FAR[0], FAR[1])


def pack_kernel(
    pair, wq, wk, wv, wg, wb, chain, lists_in, shift_in,
    out, near_out, same_out, sel_out,
    x, w, wb_v, chain_v, lists, shift, halves, message, near, same_v, sel_v, sem,
):
    b, _, core, head = place()
    copies = [
        pltpu.make_async_copy(lists_in, lists, sem.at[0]),
        pltpu.make_async_copy(chain, chain_v, sem.at[1]),
        pltpu.make_async_copy(shift_in, shift, sem.at[2]),
        pltpu.make_async_copy(wb, wb_v, sem.at[3]),
        pltpu.make_async_copy(pair, x, sem.at[4]),
        pltpu.make_async_copy(wq, w.at[0:32], sem.at[5]),
        pltpu.make_async_copy(wk, w.at[32:64], sem.at[6]),
        pltpu.make_async_copy(wv, w.at[64:96], sem.at[7]),
        pltpu.make_async_copy(wg, w.at[96:128], sem.at[8]),
    ]
    for copy in copies:
        copy.start()
    copies[0].wait()
    copies[1].wait()
    b0, b1 = lists[0, b], lists[1, b]
    c0 = jnp.broadcast_to(chain_v[:, pl.ds(pl.multiple_of(b0 // 2 * 128, 128), 128)].astype(F32), (Q, 128))
    c1 = jnp.broadcast_to(chain_v[:, pl.ds(pl.multiple_of(b1 // 2 * 128, 128), 128)].astype(F32), (Q, 128))
    c0 = jnp.where(b0 % 2 == 0, c0, pltpu.roll(c0, 64, 1))
    c1 = jnp.where(b1 % 2 == 1, c1, pltpu.roll(c1, 64, 1))
    key_chain = jnp.where(iota((Q, 128), 1) < 64, c0, c1)
    own = jnp.where(b0 == b, 0, 64)
    p = iota((Q, 128), 0)
    sel = iota((Q, 128), 1) == own + (FIRST_OUT + p // 2) % 16 * 4 + p % 2 * 2 + core
    query_chain = jnp.sum(jnp.where(sel, key_chain, 0.0), axis=-1, keepdims=True)
    same_v[...] = (query_chain == key_chain).astype(F32)
    sel_v[...] = sel.astype(BF16)
    sent = [
        pltpu.make_async_copy(same_v, same_out, sem.at[9]),
        pltpu.make_async_copy(sel_v, sel_out, sem.at[10]),
    ]
    for copy in sent:
        copy.start()
    for copy in copies[2:]:
        copy.wait()
    s = jnp.broadcast_to(shift[...], (16, 128))
    hi = s.astype(BF16).astype(F32)
    mid = (s - hi).astype(BF16).astype(F32)
    low = s - hi - mid
    wide = jnp.broadcast_to(wb_v[...].astype(F32), (16, 128))
    row = iota((16, 128), 0)
    part = row // 4
    small = jnp.where(part == 0, wide, jnp.where(part == 1, hi, jnp.where(part == 2, mid, low)))
    small = jnp.where(row % 4 == head, small, 0.0).astype(BF16)
    w_part = w[pl.ds(pl.multiple_of(b * 16, 16), 16), :]
    flat = x[...].reshape(128, N)
    halves[0] = flat
    for c in range(4):
        halves[1, :, c * 128 : (c + 1) * 128] = pltpu.roll(flat[:, c * 128 : (c + 1) * 128].astype(F32), 64, 1).astype(BF16)
    lane = iota((128, 128), 1)

    def listed(d):
        b0, b1 = lists[0, d], lists[1, d]
        first = halves[b0 % 2, :, pl.ds(pl.multiple_of(b0 // 2 * 128, 128), 128)]
        second = halves[1 - b1 % 2, :, pl.ds(pl.multiple_of(b1 // 2 * 128, 128), 128)]
        return jnp.where(lane < 64, first, second)

    near[0:128] = listed(b)
    near[128:144] = small
    sent.append(pltpu.make_async_copy(near, near_out, sem.at[19]))
    sent[-1].start()
    away = far()
    for n in range(8):
        keys = listed(n ^ away)
        start = 2 * n * MSG
        for y in range(2):
            at = start + y * MSG
            message[at : at + 64] = keys[y * 64 : (y + 1) * 64]
            message[at + 64 : at + 80] = w_part
        span = pl.ds(start, 2 * MSG)
        sent.append(pltpu.make_async_copy(message.at[span], out.at[span], sem.at[11 + n]))
        sent[-1].start()
    for copy in sent:
        copy.wait()


def heads_small(near):
    return sum(near[k, 128:144, :].astype(F32) for k in range(HEADS))


def bias_kernel(near, out):
    core = place()[2]
    small = heads_small(near).astype(BF16)
    found = []
    for y in range(2):
        rows = pl.ds(pl.multiple_of((2 * y + core) * 32, 32), 32)
        found.append(nn(small, jnp.concatenate([near[k, rows, :] for k in range(HEADS)], axis=0))[0:4])
    tile = jnp.concatenate(found * 2, axis=0).astype(BF16)
    for r in range(8):
        out[r * 16 : (r + 1) * 16, :] = tile


def score_kernel(g, near, same, sel, s_out, v_out, gate_out, moved_out, zq_scr, k_scr):
    small = heads_small(near)
    scale = 1.0 / math.sqrt(HD)
    selector = sel[...]
    away = far()
    w = [
        jnp.concatenate([g[k % 2, 2 * (s ^ away) + k // 2, 64:80, :] for k in range(HEADS) for s in (2 * t, 2 * t + 1)], axis=0)
        for t in range(4)
    ]
    w_kv = jnp.concatenate([w[1], w[2]], axis=0)
    w_qg = jnp.concatenate([w[0], w[3]], axis=0)
    for i in range(I):
        s, t = i // 2, i % 2
        zt = jnp.concatenate([g[k % 2, 2 * s + k // 2, t * 32 : (t + 1) * 32, :] for k in range(HEADS)], axis=0)
        kv = nn(w_kv, zt).astype(BF16)
        k_scr[i] = kv[0:128]
        v_out[i] = kv[128:256]
        zq_scr[i * Q : (i + 1) * Q] = nt(selector, zt).astype(BF16)
    qg = nt(zq_scr[...], w_qg).astype(BF16)
    gate_out[...] = jax.nn.sigmoid(qg[:, 128:256].astype(F32))
    head_of_lane = iota((Q, 128), 1) // HD
    moved_out[...] = jnp.concatenate(
        [same[...] * (small[4 + k : 5 + k] + small[8 + k : 9 + k] + small[12 + k : 13 + k]) for k in range(HEADS)], axis=0
    )
    for i in range(I):
        q = qg[i * Q : (i + 1) * Q, 0:128]
        zero = jnp.zeros_like(q)
        q_all = jnp.concatenate([jnp.where(head_of_lane == k, q, zero) for k in range(HEADS)], axis=0)
        s_out[i] = nn(q_all, k_scr[i]) * scale


def mix_kernel(bias, s_in, v, gate, moved, w_out, out, acc):
    row = iota((128, 128), 0)
    n = (row % Q // 2 + FIRST_OUT - FIRST_BIAS + 16) % 16
    perm = (iota((128, 128), 1) == (2 * n + row % 2) * 4 + row // Q).astype(BF16)
    head_of_lane = iota((Q, 128), 1) // HD
    logit_bias = nn(perm, bias[...]) + moved[...]
    away = far()
    for i in range(I):
        s = s_in[i] + logit_bias
        e = jnp.exp(s - jnp.max(s, axis=-1, keepdims=True))
        p = (e * (1.0 / jnp.sum(e, axis=-1, keepdims=True))).astype(BF16)
        every = nt(p, v[i])
        o = every[0:Q]
        for k in range(1, HEADS):
            o = jnp.where(head_of_lane == k, every[k * Q : (k + 1) * Q], o)
        acc[pl.ds((i // 2 ^ away) * 2 + i % 2, Q, stride=I), :] = gate[i * Q : (i + 1) * Q, :] * o
    out[...] = nn(acc[...].astype(BF16), w_out[...]).astype(BF16)


def order_kernel(moved, out, before, after, stage, sem):
    before[...] = moved[...].astype(F32)
    turn, left = 2 * FIRST_OUT, 32 - 2 * FIRST_OUT
    copies = []
    for s in range(8):
        for t in range(2):
            after[pl.ds(s * 64 + 2 * turn + t, left, stride=2), :] = before[pl.ds(2 * s + t, left, stride=16), :]
            after[pl.ds(s * 64 + t, turn, stride=2), :] = before[pl.ds(left * 16 + 2 * s + t, turn, stride=16), :]
        span = pl.ds(s * 64, 64)
        stage[span, :] = after[span, :].astype(BF16)
        copies.append(pltpu.make_async_copy(stage.at[span], out.at[span], sem.at[s]))
        copies[-1].start()
    for copy in copies:
        copy.wait()


def call(kernel, ins, outs, scratch=(), flops=0, nbytes=0):
    return pl.pallas_call(
        kernel,
        in_specs=ins,
        out_specs=[VMEM] * len(outs) if isinstance(outs, list) else VMEM,
        out_shape=outs,
        scratch_shapes=list(scratch),
        compiler_params=pltpu.CompilerParams(vmem_limit_bytes=LIMIT),
        cost_estimate=pl.CostEstimate(flops=flops, bytes_accessed=nbytes, transcendentals=0),
    )


def local(pair, w_query, w_key, w_value, w_gate, w_bias, w_out, shift, block_lists, chain_ids):
    shape = jax.ShapeDtypeStruct
    packed, near, same, sel = pl.pallas_call(
        pack_kernel,
        in_specs=[HBM] * 9,
        out_specs=[HBM] * 4,
        out_shape=[shape((16 * MSG, 128), BF16), shape((NEAR, 128), BF16), shape((Q, 128), F32), shape((Q, 128), BF16)],
        scratch_shapes=[
            pltpu.VMEM((4, 32, N), BF16),
            pltpu.VMEM((128, 128), BF16),
            pltpu.VMEM((1, 128), BF16),
            pltpu.VMEM((1, N), jnp.int32),
            pltpu.SMEM((2, 8), jnp.int32),
            pltpu.VMEM((1, 1), F32),
            pltpu.VMEM((2, 128, N), BF16),
            pltpu.VMEM((16 * MSG, 128), BF16),
            pltpu.VMEM((NEAR, 128), BF16),
            pltpu.VMEM((Q, 128), F32),
            pltpu.VMEM((Q, 128), BF16),
            pltpu.SemaphoreType.DMA((20,)),
        ],
        cost_estimate=pl.CostEstimate(flops=0, bytes_accessed=1000000, transcendentals=0),
    )(
        pair.transpose(0, 2, 1), w_query.T, w_key.T, w_value.T, w_gate.T, w_bias.T,
        chain_ids.reshape(1, N), block_lists.T, shift.reshape(1, 1),
    )
    got = lax.all_to_all(
        packed.reshape(16, MSG, 128), ("row", "head"), 0, 0, tiled=True, axis_index_groups=OVER_BLOCK
    )
    g = lax.all_gather(got, "head", axis=0, axis_index_groups=OVER_CORE)
    near = lax.all_gather(near, "head", axis=0)
    mine = call(bias_kernel, [VMEM], shape((128, 128), BF16), nbytes=400000)(near)
    bias = lax.all_to_all(
        mine.reshape(16, 8, 128), ("row", "head"), 0, 0, tiled=True, axis_index_groups=along_z(FIRST_BIAS, False)
    ).reshape(128, 128)
    scores, v, gate, moved = call(
        score_kernel,
        [VMEM] * 4,
        [shape((I, 128, 128), F32), shape((I, 128, 128), BF16), shape((I * Q, 128), F32), shape((128, 128), F32)],
        [pltpu.VMEM((I * Q, 128), BF16), pltpu.VMEM((I, 128, 128), BF16)],
        flops=1000000000,
        nbytes=4000000,
    )(g, near, same, sel)
    mixed = call(
        mix_kernel,
        [VMEM] * 6,
        shape((I * Q, 128), BF16),
        [pltpu.VMEM((I * Q, 128), F32)],
        flops=100000000,
        nbytes=3000000,
    )(bias, scores, v, gate, moved, w_out)
    arrived = lax.all_to_all(
        mixed.reshape(32, I, 128), ("row", "head"), 0, 0, tiled=True, axis_index_groups=along_z(FIRST_OUT, True)
    ).reshape(512, 128)
    ordered = pl.pallas_call(
        order_kernel,
        in_specs=[VMEM],
        out_specs=HBM,
        out_shape=shape((512, 128), BF16),
        scratch_shapes=[
            pltpu.VMEM((512, 128), F32),
            pltpu.VMEM((512, 128), F32),
            pltpu.VMEM((512, 128), BF16),
            pltpu.SemaphoreType.DMA((8,)),
        ],
        compiler_params=pltpu.CompilerParams(vmem_limit_bytes=LIMIT),
        cost_estimate=pl.CostEstimate(flops=0, bytes_accessed=300000, transcendentals=0),
    )(arrived)
    return ordered.reshape(512, 1, 128)


def solution(mesh):
    in_specs = (
        P("row", None, "head"),
        P(None, "head"),
        P(None, "head"),
        P(None, "head"),
        P(None, "head"),
        P(None, "head"),
        P(),
        P("head"),
        P(),
        P(),
    )
    out_specs = P(None, ("row", "head"), None)
    return jax.shard_map(local, mesh=mesh, in_specs=in_specs, out_specs=out_specs, check_vma=False)
```

```python
import math

import jax
import jax.numpy as jnp
import numpy as np
from jax import lax
from jax.experimental import pallas as pl
from jax.experimental.pallas import tpu as pltpu
from jax.sharding import PartitionSpec as P

F32, BF16 = jnp.float32, jnp.bfloat16
VMEM = pl.BlockSpec(memory_space=pltpu.VMEM)
HBM = pl.BlockSpec(memory_space=pltpu.HBM)
LIMIT = 24 * 1024 * 1024
HEADS, HD, N = 4, 32, 512
DEVICES = np.arange(512).reshape(8, 16, 2, 2)
FAR = [0] + [6] * 15
OVER_BLOCK = [
    group
    for z in range(16)
    for group in DEVICES[np.arange(8) ^ FAR[z], z].transpose(2, 0, 1).reshape(2, 16).tolist()
]
FIRST_BIAS, FIRST_OUT = 11, 8


def along_z(first, with_y):
    order = DEVICES[:, (first + np.arange(16)) % 16]
    return (order.transpose(0, 3, 1, 2).reshape(16, 32) if with_y else order.transpose(0, 2, 3, 1).reshape(32, 16)).tolist()


OVER_CORE = [[0, 1], [2, 3]]
Q, I = 32, 16
MSG = 80
NEAR = 144


def nt(a, b):
    return lax.dot_general(a, b, (((1,), (1,)), ((), ())), preferred_element_type=F32)


def nn(a, b):
    return jnp.dot(a, b, preferred_element_type=F32)


def iota(shape, dim):
    return lax.broadcasted_iota(jnp.int32, shape, dim)


def place():
    row, head = lax.axis_index("row"), lax.axis_index("head")
    return row // 16, head // 2, head % 2, head


def far():
    return jnp.where(lax.axis_index("row") % 16 == 0, FAR[0], FAR[1])


def pack_kernel(
    pair, wq, wk, wv, wg, wb, chain, lists_in, shift_in,
    out, near_out, same_out, sel_out,
    x, w, wb_v, chain_v, lists, shift, halves, message, near, same_v, sel_v, sem,
):
    b, _, core, head = place()
    copies = [
        pltpu.make_async_copy(lists_in, lists, sem.at[0]),
        pltpu.make_async_copy(chain, chain_v, sem.at[1]),
        pltpu.make_async_copy(shift_in, shift, sem.at[2]),
        pltpu.make_async_copy(wb, wb_v, sem.at[3]),
        pltpu.make_async_copy(pair, x, sem.at[4]),
        pltpu.make_async_copy(wq, w.at[0:32], sem.at[5]),
        pltpu.make_async_copy(wk, w.at[32:64], sem.at[6]),
        pltpu.make_async_copy(wv, w.at[64:96], sem.at[7]),
        pltpu.make_async_copy(wg, w.at[96:128], sem.at[8]),
    ]
    for copy in copies:
        copy.start()
    copies[0].wait()
    copies[1].wait()
    b0, b1 = lists[0, b], lists[1, b]
    c0 = jnp.broadcast_to(chain_v[:, pl.ds(pl.multiple_of(b0 // 2 * 128, 128), 128)].astype(F32), (Q, 128))
    c1 = jnp.broadcast_to(chain_v[:, pl.ds(pl.multiple_of(b1 // 2 * 128, 128), 128)].astype(F32), (Q, 128))
    c0 = jnp.where(b0 % 2 == 0, c0, pltpu.roll(c0, 64, 1))
    c1 = jnp.where(b1 % 2 == 1, c1, pltpu.roll(c1, 64, 1))
    key_chain = jnp.where(iota((Q, 128), 1) < 64, c0, c1)
    own = jnp.where(b0 == b, 0, 64)
    p = iota((Q, 128), 0)
    sel = iota((Q, 128), 1) == own + (FIRST_OUT + p // 2) % 16 * 4 + p % 2 * 2 + core
    query_chain = jnp.sum(jnp.where(sel, key_chain, 0.0), axis=-1, keepdims=True)
    same_v[...] = (query_chain == key_chain).astype(F32)
    sel_v[...] = sel.astype(BF16)
    sent = [
        pltpu.make_async_copy(same_v, same_out, sem.at[9]),
        pltpu.make_async_copy(sel_v, sel_out, sem.at[10]),
    ]
    for copy in sent:
        copy.start()
    for copy in copies[2:]:
        copy.wait()
    s = jnp.broadcast_to(shift[...], (16, 128))
    hi = s.astype(BF16).astype(F32)
    mid = (s - hi).astype(BF16).astype(F32)
    low = s - hi - mid
    wide = jnp.broadcast_to(wb_v[...].astype(F32), (16, 128))
    row = iota((16, 128), 0)
    part = row // 4
    small = jnp.where(part == 0, wide, jnp.where(part == 1, hi, jnp.where(part == 2, mid, low)))
    small = jnp.where(row % 4 == head, small, 0.0).astype(BF16)
    w_part = w[pl.ds(pl.multiple_of(b * 16, 16), 16), :]
    flat = x[...].reshape(128, N)
    halves[0] = flat
    for c in range(4):
        halves[1, :, c * 128 : (c + 1) * 128] = pltpu.roll(flat[:, c * 128 : (c + 1) * 128].astype(F32), 64, 1).astype(BF16)
    lane = iota((128, 128), 1)

    def listed(d):
        b0, b1 = lists[0, d], lists[1, d]
        first = halves[b0 % 2, :, pl.ds(pl.multiple_of(b0 // 2 * 128, 128), 128)]
        second = halves[1 - b1 % 2, :, pl.ds(pl.multiple_of(b1 // 2 * 128, 128), 128)]
        return jnp.where(lane < 64, first, second)

    near[0:128] = listed(b)
    near[128:144] = small
    sent.append(pltpu.make_async_copy(near, near_out, sem.at[19]))
    sent[-1].start()
    away = far()
    for n in range(8):
        keys = listed(n ^ away)
        start = 2 * n * MSG
        for y in range(2):
            at = start + y * MSG
            message[at : at + 64] = keys[y * 64 : (y + 1) * 64]
            message[at + 64 : at + 80] = w_part
        span = pl.ds(start, 2 * MSG)
        sent.append(pltpu.make_async_copy(message.at[span], out.at[span], sem.at[11 + n]))
        sent[-1].start()
    for copy in sent:
        copy.wait()


def heads_small(near):
    return sum(near[k, 128:144, :].astype(F32) for k in range(HEADS))


def bias_kernel(near, out):
    core = place()[2]
    small = heads_small(near).astype(BF16)
    z = [
        jnp.concatenate([near[k, pl.ds(pl.multiple_of((2 * y + core) * 32, 32), 32), :] for k in range(HEADS)], axis=0)
        for y in range(2)
    ]
    both = nn(small, jnp.concatenate(z, axis=1))[0:4]
    tile = jnp.concatenate([both[:, 0:128], both[:, 128:256]] * 2, axis=0).astype(BF16)
    for r in range(8):
        out[r * 16 : (r + 1) * 16, :] = tile


def score_kernel(g, near, same, sel, s_out, v_out, gate_out, zq_scr, k_scr):
    small = heads_small(near)
    scale = 1.0 / math.sqrt(HD)
    selector = sel[...]
    away = far()
    w = [
        jnp.concatenate([g[k % 2, 2 * (s ^ away) + k // 2, 64:80, :] for k in range(HEADS) for s in (2 * t, 2 * t + 1)], axis=0)
        for t in range(4)
    ]
    w_kv = jnp.concatenate([w[1], w[2]], axis=0)
    w_qg = jnp.concatenate([w[0], w[3]], axis=0)
    for i in range(I):
        s, t = i // 2, i % 2
        zt = jnp.concatenate([g[k % 2, 2 * s + k // 2, t * 32 : (t + 1) * 32, :] for k in range(HEADS)], axis=0)
        kv = nn(w_kv, zt).astype(BF16)
        k_scr[i] = kv[0:128]
        v_out[i] = kv[128:256]
        zq_scr[i * Q : (i + 1) * Q] = nt(selector, zt).astype(BF16)
    qg = nt(zq_scr[...], w_qg).astype(BF16)
    gate_out[...] = jax.nn.sigmoid(qg[:, 128:256].astype(F32))
    head_of_lane = iota((Q, 128), 1) // HD
    moved = jnp.concatenate(
        [same[...] * (small[4 + k : 5 + k] + small[8 + k : 9 + k] + small[12 + k : 13 + k]) for k in range(HEADS)], axis=0
    )
    for i in range(I):
        q = qg[i * Q : (i + 1) * Q, 0:128]
        zero = jnp.zeros_like(q)
        q_all = jnp.concatenate([jnp.where(head_of_lane == k, q, zero) for k in range(HEADS)], axis=0)
        s_out[i] = nn(q_all, k_scr[i]) * scale + moved


def mix_kernel(bias, s_in, v, gate, w_out, out, acc):
    row = iota((128, 128), 0)
    n = (row % Q // 2 + FIRST_OUT - FIRST_BIAS + 16) % 16
    perm = (iota((128, 128), 1) == (2 * n + row % 2) * 4 + row // Q).astype(BF16)
    head_of_lane = iota((Q, 128), 1) // HD
    plane = nn(perm, bias[...])
    away = far()
    for i in range(I):
        s = s_in[i] + plane
        e = jnp.exp(s - jnp.max(s, axis=-1, keepdims=True))
        p = (e * (1.0 / jnp.sum(e, axis=-1, keepdims=True))).astype(BF16)
        every = nt(p, v[i])
        o = every[0:Q]
        for k in range(1, HEADS):
            o = jnp.where(head_of_lane == k, every[k * Q : (k + 1) * Q], o)
        acc[pl.ds((i // 2 ^ away) * 2 + i % 2, Q, stride=I), :] = gate[i * Q : (i + 1) * Q, :] * o
    out[...] = nn(acc[...].astype(BF16), w_out[...]).astype(BF16)


def order_kernel(moved, out, before, after, stage, sem):
    before[...] = moved[...].astype(F32)
    turn, left = 2 * FIRST_OUT, 32 - 2 * FIRST_OUT
    copies = []
    for s in range(8):
        for t in range(2):
            after[pl.ds(s * 64 + 2 * turn + t, left, stride=2), :] = before[pl.ds(2 * s + t, left, stride=16), :]
            after[pl.ds(s * 64 + t, turn, stride=2), :] = before[pl.ds(left * 16 + 2 * s + t, turn, stride=16), :]
        span = pl.ds(s * 64, 64)
        stage[span, :] = after[span, :].astype(BF16)
        copies.append(pltpu.make_async_copy(stage.at[span], out.at[span], sem.at[s]))
        copies[-1].start()
    for copy in copies:
        copy.wait()


def call(kernel, ins, outs, scratch=(), flops=0, nbytes=0):
    return pl.pallas_call(
        kernel,
        in_specs=ins,
        out_specs=[VMEM] * len(outs) if isinstance(outs, list) else VMEM,
        out_shape=outs,
        scratch_shapes=list(scratch),
        compiler_params=pltpu.CompilerParams(vmem_limit_bytes=LIMIT),
        cost_estimate=pl.CostEstimate(flops=flops, bytes_accessed=nbytes, transcendentals=0),
    )


def local(pair, w_query, w_key, w_value, w_gate, w_bias, w_out, shift, block_lists, chain_ids):
    shape = jax.ShapeDtypeStruct
    packed, near, same, sel = pl.pallas_call(
        pack_kernel,
        in_specs=[HBM] * 9,
        out_specs=[HBM] * 4,
        out_shape=[shape((16 * MSG, 128), BF16), shape((NEAR, 128), BF16), shape((Q, 128), F32), shape((Q, 128), BF16)],
        scratch_shapes=[
            pltpu.VMEM((4, 32, N), BF16),
            pltpu.VMEM((128, 128), BF16),
            pltpu.VMEM((1, 128), BF16),
            pltpu.VMEM((1, N), jnp.int32),
            pltpu.SMEM((2, 8), jnp.int32),
            pltpu.VMEM((1, 1), F32),
            pltpu.VMEM((2, 128, N), BF16),
            pltpu.VMEM((16 * MSG, 128), BF16),
            pltpu.VMEM((NEAR, 128), BF16),
            pltpu.VMEM((Q, 128), F32),
            pltpu.VMEM((Q, 128), BF16),
            pltpu.SemaphoreType.DMA((20,)),
        ],
        cost_estimate=pl.CostEstimate(flops=0, bytes_accessed=1000000, transcendentals=0),
    )(
        pair.transpose(0, 2, 1), w_query.T, w_key.T, w_value.T, w_gate.T, w_bias.T,
        chain_ids.reshape(1, N), block_lists.T, shift.reshape(1, 1),
    )
    got = lax.all_to_all(
        packed.reshape(16, MSG, 128), ("row", "head"), 0, 0, tiled=True, axis_index_groups=OVER_BLOCK
    )
    g = lax.all_gather(got, "head", axis=0, axis_index_groups=OVER_CORE)
    near = lax.all_gather(near, "head", axis=0)
    mine = call(bias_kernel, [VMEM], shape((128, 128), BF16), nbytes=400000)(near)
    bias = lax.all_to_all(
        mine.reshape(16, 8, 128), ("row", "head"), 0, 0, tiled=True, axis_index_groups=along_z(FIRST_BIAS, False)
    ).reshape(128, 128)
    scores, v, gate = call(
        score_kernel,
        [VMEM] * 4,
        [shape((I, 128, 128), F32), shape((I, 128, 128), BF16), shape((I * Q, 128), F32)],
        [pltpu.VMEM((I * Q, 128), BF16), pltpu.VMEM((I, 128, 128), BF16)],
        flops=1000000000,
        nbytes=4000000,
    )(g, near, same, sel)
    mixed = call(
        mix_kernel,
        [VMEM] * 5,
        shape((I * Q, 128), BF16),
        [pltpu.VMEM((I * Q, 128), F32)],
        flops=100000000,
        nbytes=3000000,
    )(bias, scores, v, gate, w_out)
    moved = lax.all_to_all(
        mixed.reshape(32, I, 128), ("row", "head"), 0, 0, tiled=True, axis_index_groups=along_z(FIRST_OUT, True)
    ).reshape(512, 128)
    ordered = pl.pallas_call(
        order_kernel,
        in_specs=[VMEM],
        out_specs=HBM,
        out_shape=shape((512, 128), BF16),
        scratch_shapes=[
            pltpu.VMEM((512, 128), F32),
            pltpu.VMEM((512, 128), F32),
            pltpu.VMEM((512, 128), BF16),
            pltpu.SemaphoreType.DMA((8,)),
        ],
        compiler_params=pltpu.CompilerParams(vmem_limit_bytes=LIMIT),
        cost_estimate=pl.CostEstimate(flops=0, bytes_accessed=300000, transcendentals=0),
    )(moved)
    return ordered.reshape(512, 1, 128)


def solution(mesh):
    in_specs = (
        P("row", None, "head"),
        P(None, "head"),
        P(None, "head"),
        P(None, "head"),
        P(None, "head"),
        P(None, "head"),
        P(),
        P("head"),
        P(),
        P(),
    )
    out_specs = P(None, ("row", "head"), None)
    return jax.shard_map(local, mesh=mesh, in_specs=in_specs, out_specs=out_specs, check_vma=False)
```
